32 devices in a mesh: guide: 2 (over core), kv: 4 (over y, x), seq: 4 (over z).
Axes of the slice: x: 2, y: 2, z: 4, core: 2. Of those that a mesh axis runs over, the one named last changes fastest.
Arguments:
- hidden: bfloat16 [2, 8, 4608], P(None, None, ('guide', 'seq')), may hold values from -50 to 50
- lengths: int32 [2, 8], replicated, may hold values from 1 to 8192, as said below
- slot_owner: int32 [2, 8], replicated, may hold values from 0 to 7, each once within a row
- allowed_ids: int32 [65536], P(('kv', 'seq')), may hold values from 0 to 131071, as said below
- guidance: float32 [8], replicated, may hold values from 1 to 4
- pre_attn_gain: float32 [4608], P(('guide', 'seq')), may hold values from 0.1 to 1.9
- post_attn_gain: float32 [4608], P(('guide', 'seq')), may hold values from 0.4 to 2.1
- pre_ffw_gain: float32 [4608], P(('guide', 'seq')), may hold values from 0.1 to 1.9
- post_ffw_gain: float32 [4608], P(('guide', 'seq')), may hold values from 0.4 to 2.1
- final_gain: float32 [4608], P(('guide', 'seq')), may hold values from 0.1 to 1.9
- query_weight: bfloat16 [4608, 4096], P(('guide', 'seq'), 'kv'), may hold values from -0.09375 to 0.09375
- key_weight: bfloat16 [4608, 2048], P(('guide', 'seq'), 'kv'), may hold values from -0.09375 to 0.09375
- value_weight: bfloat16 [4608, 2048], P(('guide', 'seq'), 'kv'), may hold values from -0.09375 to 0.09375
- output_weight: bfloat16 [4096, 4608], P('kv', ('guide', 'seq')), may hold values from -1 to 1
- gate_weight: bfloat16 [4608, 36864], P(('guide', 'seq'), 'kv'), may hold values from -1 to 1
- up_weight: bfloat16 [4608, 36864], P(('guide', 'seq'), 'kv'), may hold values from -1 to 1
- down_weight: bfloat16 [36864, 4608], P('kv', ('guide', 'seq')), may hold values from -1 to 1
- embedding: bfloat16 [131072, 4608], P(('kv', 'seq'), 'guide'), may hold values from -1 to 1
- cond_keys: bfloat16 [8, 8192, 2048], P(None, ('guide', 'seq'), 'kv'), may hold values from -6 to 6
- cond_values: bfloat16 [8, 8192, 2048], P(None, ('guide', 'seq'), 'kv'), may hold values from -6 to 6
- uncond_keys: bfloat16 [8, 2048, 2048], P(None, ('guide', 'seq'), 'kv'), may hold values from -6 to 6
- uncond_values: bfloat16 [8, 2048, 2048], P(None, ('guide', 'seq'), 'kv'), may hold values from -6 to 6
Outputs:
- mixed: float32 [8, 65536], P('guide', ('kv', 'seq'))
The draws below stay inside these ranges and needn't reach their ends.
Inputs may be any that keep to these rules, and one draw needn't show every extreme that they name: lengths[0] lies in 1 to 8192 and some request has exactly 8192; lengths[1] lies in 1 to 2048 and some request has exactly 2048. `slot_owner`: each row is a permutation of the 8 requests. `allowed_ids`: the ids of the i-th aligned block of 4096 entries are distinct and lie in rows i * 8192 to (i + 1) * 8192 - 1 of the table.
All inputs are finite; a program needn't handle non-finite values.
Results may differ from the reference program's by a relative error of at most 0.0039.
Values may be sent and summed in bfloat16 or wider, within the bound.
No kernel may reach another device: no remote copies, remote signals or barrier semaphores. Data moves between devices by JAX's collectives and lax.ppermute only.
A program may use at most 192 MiB of HBM per device.

```python
import jax
import jax.numpy as jnp
from jax import lax

D = 4608
H = 32
KVH = 16
HD = 128
FF = 36864
VOCAB = 131072
ALLOWED = 65536
CAP = 8192
UCAP = 2048
R = 8
VBLOCKS = 16
VROWS = 8192
ABLOCK = 4096


PROFILE_RMS = 1.4662


def profile(key):
    base_key = jax.random.fold_in(key, 7001)
    size_key = jax.random.fold_in(base_key, 1)
    sign_key = jax.random.fold_in(base_key, 2)
    magnitude = 10.0 ** jax.random.uniform(size_key, (D,), dtype=jnp.float32, minval=-0.5, maxval=0.5)
    signs = jnp.where(jax.random.bernoulli(sign_key, 0.5, (D,)), 1.0, -1.0).astype(jnp.float32)
    return (magnitude, signs * magnitude / PROFILE_RMS)


def clipped_normal(key, shape, limit):
    return jnp.clip(jax.random.normal(key, shape, dtype=jnp.float32), -limit, limit)


def draw_hidden(key, part):
    magnitude, direction = profile(key)
    rough_key = jax.random.fold_in(key, 11)
    row_key = jax.random.fold_in(key, 12)
    column_scale = 10.0 ** (jnp.arange(D, dtype=jnp.float32) / D)
    row_scale = 10.0 ** jax.random.uniform(row_key, (2, R, 1), dtype=jnp.float32)
    base = jnp.clip(jax.random.normal(rough_key, (2, R, D), dtype=jnp.float32), -4.0, 4.0)
    return (row_scale * (0.1 * base * column_scale + 0.4 * direction)).astype(jnp.bfloat16)


def draw_lengths(key, part):
    cond_key = jax.random.fold_in(key, 21)
    uncond_key = jax.random.fold_in(key, 22)
    pick_key = jax.random.fold_in(key, 23)
    cond_len = jax.random.randint(cond_key, (R,), 1, CAP + 1)
    uncond_len = jax.random.randint(uncond_key, (R,), 1, UCAP + 1)
    picked = jax.random.randint(pick_key, (2,), 0, R)
    places = jnp.arange(R, dtype=jnp.int32)
    cond_len = jnp.where(places == picked[0], CAP, cond_len)
    uncond_len = jnp.where(places == picked[1], UCAP, uncond_len)
    return jnp.stack([cond_len, uncond_len]).astype(jnp.int32)


def draw_allowed_ids(key, part):
    noise = jax.random.randint(jax.random.fold_in(key, 31), (VBLOCKS, VROWS), 0, (1 << 30) // VROWS)
    local_rows = jnp.arange(VROWS, dtype=jnp.int32)
    scores = noise * VROWS + local_rows[None, :]
    scores = jnp.where(local_rows[None, :] == 0, -2, scores)
    scores = jnp.where(local_rows[None, :] == VROWS - 1, -1, scores)
    order = jnp.argsort(scores, axis=1)[:, :ABLOCK].astype(jnp.int32)
    block_first = (jnp.arange(VBLOCKS, dtype=jnp.int32) * VROWS)[:, None]
    return (order + block_first).reshape(ALLOWED).astype(jnp.int32)


def draw_post_attn_gain(key, part):
    magnitude, direction = profile(key)
    jitter = jax.random.uniform(jax.random.fold_in(key, 41), (D,), dtype=jnp.float32, minval=0.8, maxval=1.2)
    return (0.35 + 0.45 * magnitude * jitter).astype(jnp.float32)


def draw_post_ffw_gain(key, part):
    magnitude, direction = profile(key)
    jitter = jax.random.uniform(jax.random.fold_in(key, 42), (D,), dtype=jnp.float32, minval=0.8, maxval=1.2)
    return (0.35 + 0.45 * magnitude * jitter).astype(jnp.float32)


def draw_output_weight(key, part):
    magnitude, direction = profile(key)
    rough_key = jax.random.fold_in(key, 51)
    shared_key = jax.random.fold_in(key, 52)
    rough = clipped_normal(rough_key, (H * HD, D), 4.0)
    shared = clipped_normal(shared_key, (1, D), 3.0)
    column = (magnitude / PROFILE_RMS)[None, :]
    return (column * (rough + shared) * (2 * H * HD) ** (-0.5)).astype(jnp.bfloat16)


def unit_pair(key):
    first = clipped_normal(jax.random.fold_in(key, 61), (D, FF), 4.0)
    second = clipped_normal(jax.random.fold_in(key, 62), (D, FF), 4.0)
    return (first, second)


def draw_gate_weight(key, part):
    first, second = unit_pair(key)
    return (first * D ** (-0.5)).astype(jnp.bfloat16)


def draw_up_weight(key, part):
    first, second = unit_pair(key)
    return ((0.7 * first + 0.714 * second) * D ** (-0.5)).astype(jnp.bfloat16)


def draw_down_weight(key, part):
    magnitude, direction = profile(key)
    rough = clipped_normal(jax.random.fold_in(key, 71), (FF, D), 4.0)
    return ((rough + 2.0 * FF ** (-0.5) * direction[None, :]) * FF ** (-0.5)).astype(jnp.bfloat16)


def draw_embedding(key, part):
    magnitude, direction = profile(key)
    rough_key = jax.random.fold_in(key, 81)
    lean_key = jax.random.fold_in(key, 82)
    rough = clipped_normal(rough_key, (VOCAB, D), 4.0)
    lean = 0.15 * clipped_normal(lean_key, (VOCAB, 1), 4.0)
    return ((rough + lean * direction[None, :]) * D ** (-0.5)).astype(jnp.bfloat16)


def block_scale(key, dims, pieces, least, largest):
    def one(dim, blocks):
        draws = jax.random.uniform(jax.random.fold_in(jax.random.fold_in(key, 6), dim), (blocks,), jnp.float32, least / len(pieces), largest / len(pieces))
        return jnp.repeat(jnp.exp(draws), dims[dim] // blocks).reshape((-1,) + (1,) * (len(dims) - dim - 1))

    loudness = one(*pieces[0])
    for cut in pieces[1:]:
        loudness = loudness * one(*cut)
    return loudness


def centred(own_key, dims, scale, bound, shards=(), kind=jnp.bfloat16):
    loudness = block_scale(own_key, dims, shards, -0.22, 0.18) if shards else 1.0
    array = jax.random.normal(own_key, dims, jnp.float32) * scale * loudness
    return jnp.minimum(jnp.maximum(array, -bound), bound).astype(kind)


def setup_inputs(seed: int = 0) -> dict:
    splits = jax.random.split(jax.random.key(seed), 23)
    hidden = draw_hidden(jax.random.fold_in(splits[22], 71), 0)
    lengths = draw_lengths(jax.random.fold_in(splits[22], 71), 0)
    slot_owner = jax.vmap(lambda own: jax.random.permutation(own, R))(jax.random.split(splits[2], 2)).reshape((2, R)).astype(jnp.int32)
    allowed_ids = draw_allowed_ids(jax.random.fold_in(splits[22], 71), 0)
    guidance = jnp.clip(jax.random.uniform(splits[4], (R,), jnp.float32, 1.0, 4.0), 1.0, 4.0)
    pre_attn_gain = jnp.clip(1.0 + 0.18 * jax.random.normal(splits[5], (D,), jnp.float32), 0.1, 1.9)
    post_attn_gain = draw_post_attn_gain(jax.random.fold_in(splits[22], 71), 0)
    pre_ffw_gain = jnp.clip(1.0 + 0.18 * jax.random.normal(splits[7], (D,), jnp.float32), 0.1, 1.9)
    post_ffw_gain = draw_post_ffw_gain(jax.random.fold_in(splits[22], 71), 0)
    final_gain = jnp.clip(1.0 + 0.18 * jax.random.normal(splits[9], (D,), jnp.float32), 0.1, 1.9)
    query_weight = centred(splits[10], (D, H * HD), D ** -0.5, 0.09375, ((0, 8), (1, 4)))
    key_weight = centred(splits[11], (D, KVH * HD), D ** -0.5, 0.09375, ((0, 8), (1, 4)))
    value_weight = centred(splits[12], (D, KVH * HD), D ** -0.5, 0.09375, ((0, 8), (1, 4)))
    output_weight = draw_output_weight(jax.random.fold_in(splits[22], 71), 0)
    gate_weight = draw_gate_weight(jax.random.fold_in(splits[22], 71), 0)
    up_weight = draw_up_weight(jax.random.fold_in(splits[22], 71), 0)
    down_weight = draw_down_weight(jax.random.fold_in(splits[22], 71), 0)
    embedding = draw_embedding(jax.random.fold_in(splits[22], 71), 0)
    cond_keys = centred(splits[18], (R, CAP, KVH * HD), 1.0, 6.0, ((1, 8), (2, 4)))
    cond_values = centred(splits[19], (R, CAP, KVH * HD), 1.0, 6.0, ((1, 8), (2, 4)))
    uncond_keys = centred(splits[20], (R, UCAP, KVH * HD), 1.0, 6.0, ((1, 8), (2, 4)))
    uncond_values = centred(splits[21], (R, UCAP, KVH * HD), 1.0, 6.0, ((1, 8), (2, 4)))
    return {"hidden": hidden, "lengths": lengths, "slot_owner": slot_owner, "allowed_ids": allowed_ids, "guidance": guidance, "pre_attn_gain": pre_attn_gain, "post_attn_gain": post_attn_gain, "pre_ffw_gain": pre_ffw_gain, "post_ffw_gain": post_ffw_gain, "final_gain": final_gain, "query_weight": query_weight, "key_weight": key_weight, "value_weight": value_weight, "output_weight": output_weight, "gate_weight": gate_weight, "up_weight": up_weight, "down_weight": down_weight, "embedding": embedding, "cond_keys": cond_keys, "cond_values": cond_values, "uncond_keys": uncond_keys, "uncond_values": uncond_values}


EPS = 1e-06
ATTN_CAP = 50.0
LOGIT_CAP = 30.0
THETA = 10000.0

def rotary(values, position):
    half_size = values.shape[-1] // 2
    frequency = THETA ** (-2.0 * jnp.arange(half_size, dtype=jnp.float32) / values.shape[-1])
    angles = position[:, None, None] * frequency
    first_half = values[..., :half_size]
    second_half = values[..., half_size:]
    cosine = jnp.cos(angles)
    sine_part = jnp.sin(angles)
    return jnp.concatenate([first_half * cosine - second_half * sine_part, second_half * cosine + first_half * sine_part], axis=-1)

def reference(hidden, lengths, slot_owner, allowed_ids, guidance, pre_attn_gain, post_attn_gain, pre_ffw_gain, post_ffw_gain, final_gain, query_weight, key_weight, value_weight, output_weight, gate_weight, up_weight, down_weight, embedding, cond_keys, cond_values, uncond_keys, uncond_values):
    streams = hidden.astype(jnp.float32).reshape(2 * R, D)
    square_sum = lax.optimization_barrier(jnp.sum(streams * streams, axis=-1))
    row_scale = lax.rsqrt(square_sum / D + EPS)[:, None]
    normed = (streams * pre_attn_gain).astype(jnp.bfloat16)
    position = lengths.astype(jnp.float32).reshape(2 * R)
    query_full = jnp.dot(normed, query_weight, preferred_element_type=jnp.float32) * row_scale
    key_full = jnp.dot(normed, key_weight, preferred_element_type=jnp.float32) * row_scale
    value_full = jnp.dot(normed, value_weight, preferred_element_type=jnp.float32) * row_scale
    queries = (rotary(query_full.reshape(2 * R, H, HD), position) * (D // H) ** (-0.5)).astype(jnp.bfloat16)
    new_keys = rotary(key_full.reshape(2 * R, KVH, HD), position).astype(jnp.bfloat16)
    new_values = value_full.reshape(2 * R, KVH, HD).astype(jnp.bfloat16)
    inverse = jnp.argsort(slot_owner, axis=1).astype(jnp.int32)
    group_size = H // KVH

    def make_stream(kind, key_cache, value_cache):
        span = key_cache.shape[1]

        def one_stream(request):
            index = kind * R + request
            slot = inverse[kind, request]
            key_rows = key_cache[slot].astype(jnp.float32).reshape(span, KVH, HD)
            value_rows = value_cache[slot].astype(jnp.float32).reshape(span, KVH, HD)
            query = queries[index].astype(jnp.float32).reshape(KVH, group_size, HD)
            scores = jnp.einsum('kgd,tkd->kgt', query, key_rows)
            visible = jnp.arange(span, dtype=jnp.int32) < lengths[kind, request]
            probs = jnp.where(visible[None, None, :], jnp.exp(ATTN_CAP * jnp.tanh(scores / ATTN_CAP)), 0.0)
            rounded = lax.optimization_barrier(probs.astype(jnp.bfloat16)).astype(jnp.float32)
            numer = jnp.einsum('kgt,tkd->kgd', rounded, value_rows)
            own_score = jnp.einsum('kgd,kd->kg', query, new_keys[index].astype(jnp.float32))
            own_prob = jnp.exp(ATTN_CAP * jnp.tanh(own_score / ATTN_CAP))
            own_round = lax.optimization_barrier(own_prob.astype(jnp.bfloat16)).astype(jnp.float32)
            numer = numer + own_round[:, :, None] * new_values[index].astype(jnp.float32)[:, None, :]
            denom = lax.optimization_barrier(jnp.sum(probs, axis=-1)) + own_prob
            return (numer / denom[:, :, None]).astype(jnp.bfloat16).reshape(H * HD)
        return one_stream
    cond_att = lax.map(make_stream(0, cond_keys, cond_values), jnp.arange(R, dtype=jnp.int32))
    uncond_att = lax.map(make_stream(1, uncond_keys, uncond_values), jnp.arange(R, dtype=jnp.int32))
    attended = jnp.concatenate([cond_att, uncond_att], axis=0)
    projected = jnp.dot(attended, output_weight, preferred_element_type=jnp.float32)
    out_scale = lax.rsqrt(lax.optimization_barrier(jnp.sum(projected * projected, axis=-1)) / D + EPS)[:, None]
    middle = streams + projected * out_scale * post_attn_gain
    mid_scale = lax.rsqrt(lax.optimization_barrier(jnp.sum(middle * middle, axis=-1)) / D + EPS)[:, None]
    ffw_in = (middle * pre_ffw_gain).astype(jnp.bfloat16)
    gate = jnp.dot(ffw_in, gate_weight, preferred_element_type=jnp.float32) * mid_scale
    upward = jnp.dot(ffw_in, up_weight, preferred_element_type=jnp.float32) * mid_scale
    activ = (jax.nn.gelu(gate, approximate=True) * upward).astype(jnp.bfloat16)
    ffw_out = jnp.dot(activ, down_weight, preferred_element_type=jnp.float32)
    ffw_scale = lax.rsqrt(lax.optimization_barrier(jnp.sum(ffw_out * ffw_out, axis=-1)) / D + EPS)[:, None]
    last = middle + ffw_out * ffw_scale * post_ffw_gain
    final_scale = lax.rsqrt(lax.optimization_barrier(jnp.sum(last * last, axis=-1)) / D + EPS)[:, None]
    final_rows = (last * final_gain).astype(jnp.bfloat16)
    full_logits = jnp.dot(final_rows, embedding.T, preferred_element_type=jnp.float32)
    chosen = jnp.take(full_logits, allowed_ids, axis=1)
    logits = (LOGIT_CAP * jnp.tanh(chosen * final_scale / LOGIT_CAP)).reshape(2, R, ALLOWED)
    return logits[1] + guidance[:, None] * (logits[0] - logits[1])
```

```python
import jax
import jax.numpy as jnp
from jax import lax
from jax.experimental import pallas as pl
from jax.experimental.pallas import tpu as pltpu
from jax.sharding import PartitionSpec as P

D = 4608
H = 32
HD = 128


EPS = 1e-06
ATTN_CAP = 50.0
LOGIT_CAP = 30.0
THETA = 10000.0
HIGHEST = lax.Precision.HIGHEST


def rotary(values, position):
    half_size = values.shape[-1] // 2
    frequency = THETA ** (-2.0 * jnp.arange(half_size, dtype=jnp.float32) / values.shape[-1])
    angles = position[:, None, None] * frequency
    first_half = values[..., :half_size]
    second_half = values[..., half_size:]
    cosine = jnp.cos(angles)
    sine_part = jnp.sin(angles)
    return jnp.concatenate(
        [
            first_half * cosine - second_half * sine_part,
            second_half * cosine + first_half * sine_part,
        ],
        axis=-1,
    )


def to_slots(slot_pick, array):
    flat = array.astype(jnp.float32).reshape(array.shape[0], array.shape[1], -1)
    moved = jnp.einsum("gsr,gre->gse", slot_pick, flat, precision=HIGHEST)
    return moved.reshape(array.shape).astype(array.dtype)


def to_requests(slot_pick, array):
    flat = array.astype(jnp.float32).reshape(array.shape[0], array.shape[1], -1)
    moved = jnp.einsum("gsr,gse->gre", slot_pick, flat, precision=HIGHEST)
    return moved.reshape(array.shape).astype(array.dtype)


def attend_block(queries, key_block, value_block, slot_len, first_pos, tile_len):
    slot_count, block_len = (key_block.shape[0], key_block.shape[1])
    local_kv, group_size, head_size = (queries.shape[1], queries.shape[2], queries.shape[3])
    live_len = jnp.clip(jnp.max(slot_len) - first_pos, 0, block_len)
    tile_count = (live_len + tile_len - 1) // tile_len

    def one_tile(tile_index, carry):
        numer, denom = carry
        tile_start = tile_index * tile_len
        key_tile = lax.dynamic_slice_in_dim(key_block, tile_start, tile_len, 1).reshape(
            slot_count, tile_len, local_kv, head_size
        )
        value_tile = lax.dynamic_slice_in_dim(value_block, tile_start, tile_len, 1).reshape(
            slot_count, tile_len, local_kv, head_size
        )
        scores = jnp.einsum(
            "rkgd,rtkd->rkgt", queries, key_tile, preferred_element_type=jnp.float32
        )
        places = first_pos + tile_start + jnp.arange(tile_len, dtype=jnp.int32)
        visible = places[None, None, None, :] < slot_len[:, None, None, None]
        probs = jnp.where(visible, jnp.exp(ATTN_CAP * jnp.tanh(scores / ATTN_CAP)), 0.0)
        numer = numer + jnp.einsum(
            "rkgt,rtkd->rkgd",
            probs.astype(jnp.bfloat16),
            value_tile,
            preferred_element_type=jnp.float32,
        )
        denom = denom + jnp.sum(probs, axis=-1)
        return (numer, denom)

    start_numer = jnp.zeros((slot_count, local_kv, group_size, head_size), jnp.float32)
    start_denom = jnp.zeros((slot_count, local_kv, group_size), jnp.float32)
    return lax.fori_loop(0, tile_count, one_tile, (start_numer, start_denom))


def plain_layer(
    hidden,
    lengths,
    slot_owner,
    allowed_ids,
    guidance,
    pre_attn_gain,
    post_attn_gain,
    pre_ffw_gain,
    post_ffw_gain,
    final_gain,
    query_weight,
    key_weight,
    value_weight,
    output_weight,
    gate_weight,
    up_weight,
    down_weight,
    embedding,
    cond_keys,
    cond_values,
    uncond_keys,
    uncond_values,
):
    kinds, requests, width_local = hidden.shape
    stream_count = kinds * requests
    local_heads = query_weight.shape[1] // HD
    local_kv = key_weight.shape[1] // HD
    group_size = local_heads // local_kv
    streams = hidden.astype(jnp.float32)
    normed = (streams * pre_attn_gain).astype(jnp.bfloat16).reshape(stream_count, width_local)
    query_part = jnp.dot(normed, query_weight, preferred_element_type=jnp.float32)
    key_part = jnp.dot(normed, key_weight, preferred_element_type=jnp.float32)
    value_part = jnp.dot(normed, value_weight, preferred_element_type=jnp.float32)
    square_part = jnp.sum(streams * streams, axis=-1)
    square_sum, query_sum, key_sum, value_sum = lax.psum(
        (square_part, query_part, key_part, value_part), ("guide", "seq")
    )
    row_scale = lax.rsqrt(square_sum / D + EPS).reshape(stream_count, 1)
    position = lengths.astype(jnp.float32).reshape(stream_count)
    queries = (
        rotary((query_sum * row_scale).reshape(stream_count, local_heads, HD), position)
        * (D // H) ** (-0.5)
    ).astype(jnp.bfloat16)
    new_keys = rotary((key_sum * row_scale).reshape(stream_count, local_kv, HD), position).astype(
        jnp.bfloat16
    )
    new_values = (value_sum * row_scale).astype(jnp.bfloat16)
    queries = queries.reshape(kinds, requests, local_kv, group_size, HD)
    new_keys = new_keys.reshape(kinds, requests, local_kv, HD)
    new_values = new_values.reshape(kinds, requests, local_kv, HD)
    matches = slot_owner[:, :, None] == jnp.arange(requests, dtype=jnp.int32)[None, None, :]
    slot_pick = matches.astype(jnp.float32)
    slot_len = jnp.sum(jnp.where(matches, lengths[:, None, :], 0), axis=-1)
    slot_queries = to_slots(slot_pick, queries)
    slot_keys = to_slots(slot_pick, new_keys)
    slot_values = to_slots(slot_pick, new_values)
    guide_index = lax.axis_index("guide")
    seq_index = lax.axis_index("seq")
    block_index = guide_index * lax.axis_size("seq") + seq_index
    cond_len = cond_keys.shape[1]
    uncond_len = uncond_keys.shape[1]
    cond_numer, cond_denom = attend_block(
        slot_queries[0],
        cond_keys,
        cond_values,
        slot_len[0],
        block_index * cond_len,
        min(256, cond_len),
    )
    uncond_numer, uncond_denom = attend_block(
        slot_queries[1],
        uncond_keys,
        uncond_values,
        slot_len[1],
        block_index * uncond_len,
        min(256, uncond_len),
    )
    numer_part = jnp.stack([cond_numer, uncond_numer])
    denom_part = jnp.stack([cond_denom, uncond_denom])
    numer_sum, denom_sum = lax.psum((numer_part, denom_part), ("guide", "seq"))
    own_score = jnp.einsum(
        "gskjd,gskd->gskj", slot_queries, slot_keys, preferred_element_type=jnp.float32
    )
    own_prob = jnp.exp(ATTN_CAP * jnp.tanh(own_score / ATTN_CAP))
    own_weight = own_prob.astype(jnp.bfloat16).astype(jnp.float32)
    numer_total = (
        numer_sum + own_weight[..., None] * slot_values.astype(jnp.float32)[:, :, :, None, :]
    )
    denom_total = denom_sum + own_prob
    attended_slots = (numer_total / denom_total[..., None]).astype(jnp.bfloat16)
    attended = to_requests(slot_pick, attended_slots).reshape(stream_count, local_heads * HD)
    out_part = jnp.dot(attended, output_weight, preferred_element_type=jnp.float32)
    projected = lax.psum(out_part, "kv").reshape(kinds, requests, width_local)
    branch_sq = lax.psum(jnp.sum(projected * projected, axis=-1), ("guide", "seq"))
    out_scale = lax.rsqrt(branch_sq / D + EPS)
    middle = streams + projected * out_scale[..., None] * post_attn_gain
    middle_sq = lax.psum(jnp.sum(middle * middle, axis=-1), ("guide", "seq"))
    ffw_in = (middle * pre_ffw_gain).astype(jnp.bfloat16).reshape(stream_count, width_local)
    ffw_scale = lax.rsqrt(middle_sq / D + EPS).reshape(stream_count, 1)
    gate_part = jnp.dot(ffw_in, gate_weight, preferred_element_type=jnp.float32)
    upward_part = jnp.dot(ffw_in, up_weight, preferred_element_type=jnp.float32)
    gate_sum, upward_sum = lax.psum((gate_part, upward_part), ("guide", "seq"))
    activ = (jax.nn.gelu(gate_sum * ffw_scale, approximate=True) * (upward_sum * ffw_scale)).astype(
        jnp.bfloat16
    )
    down_part = jnp.dot(activ, down_weight, preferred_element_type=jnp.float32)
    ffw_out = lax.psum(down_part, "kv").reshape(kinds, requests, width_local)
    ffw_sq = lax.psum(jnp.sum(ffw_out * ffw_out, axis=-1), ("guide", "seq"))
    branch_scale = lax.rsqrt(ffw_sq / D + EPS)
    last = middle + ffw_out * branch_scale[..., None] * post_ffw_gain
    last_sq = lax.psum(jnp.sum(last * last, axis=-1), ("guide", "seq"))
    final_scale = lax.rsqrt(last_sq / D + EPS)
    final_rows = (last * final_gain).astype(jnp.bfloat16)
    half_rows = lax.all_gather(final_rows, "seq", axis=2, tiled=True)
    table_rows = embedding.shape[0]
    block_first = (lax.axis_index("kv") * lax.axis_size("seq") + seq_index) * table_rows
    picked = jnp.take(embedding, allowed_ids - block_first, axis=0)
    logit_part = jnp.einsum(
        "sd,ad->sa",
        half_rows.reshape(stream_count, half_rows.shape[2]),
        picked,
        preferred_element_type=jnp.float32,
    )
    logit_term = jnp.transpose(logit_part.reshape(kinds, requests, picked.shape[0]), (1, 0, 2))
    logit_share = lax.psum_scatter(logit_term, "guide", scatter_dimension=0, tiled=True)
    half_req = requests // 2
    first_req = guide_index * half_req
    share_scale = jnp.transpose(
        lax.dynamic_slice_in_dim(final_scale, first_req, half_req, 1), (1, 0)
    )
    capped = LOGIT_CAP * jnp.tanh(logit_share * share_scale[:, :, None] / LOGIT_CAP)
    share_weight = lax.dynamic_slice_in_dim(guidance, first_req, half_req, 0)
    return capped[:, 1] + share_weight[:, None] * (capped[:, 0] - capped[:, 1])


BF = jnp.bfloat16
F32 = jnp.float32
LANES = 128
VMEM = pl.BlockSpec(memory_space=pltpu.VMEM)
SMEM = pl.BlockSpec(memory_space=pltpu.SMEM)
MIB = 1 << 20


def nt_dot(a, b):
    return lax.dot_general(a, b, (((1,), (1,)), ((), ())), preferred_element_type=F32)


def nn_dot(a, b):
    return jnp.dot(a, b, preferred_element_type=F32)


def limit(mib):
    return pltpu.CompilerParams(vmem_limit_bytes=mib * MIB)


def columns_tile(values, rows):
    lane = lax.broadcasted_iota(jnp.int32, (rows, LANES), 1)
    tile = jnp.zeros((rows, LANES), F32)
    for place, value in enumerate(values):
        tile = jnp.where(lane == place, value, tile)
    return tile


def split_tile(tile):
    high = tile.astype(BF).astype(F32)
    rest = tile - high
    middle = rest.astype(BF).astype(F32)
    low = (rest - middle).astype(BF).astype(F32)
    return (high + pltpu.roll(middle, 32, 1) + pltpu.roll(low, 64, 1)).astype(BF)


def joined_tile(tile):
    terms = tile.astype(F32)
    total = terms + pltpu.roll(terms, LANES - 32, 1) + pltpu.roll(terms, LANES - 64, 1)
    lane = lax.broadcasted_iota(jnp.int32, total.shape, 1)
    return jnp.where(lane < 32, total, 0.0)


def project_kernel(meta, hidden, gain, wq, wk, wv, rows, keep, send):
    count = hidden.shape[0]
    half = count // 2
    group = half // 2
    row = lax.broadcasted_iota(jnp.int32, (count, count), 0)
    column = lax.broadcasted_iota(jnp.int32, (count, count), 1)
    source = (row // group) % 2 * half + row // half * group + row % group
    pick = jnp.where(column == source, 1.0, 0.0).astype(BF)
    streams = nn_dot(pick, hidden[...])
    rows[...] = streams.astype(BF)
    square = jnp.sum(streams * streams, axis=-1, keepdims=True)
    normed = (streams * gain[...]).astype(BF)
    first = meta[0] == 0
    offset = 0
    for weight in (wq, wk, wv):
        product = nn_dot(normed, weight[...])
        width = product.shape[1] // 2
        low, high = product[:, :width], product[:, width:]
        keep[:, offset : offset + width] = jnp.where(first, low, high)
        send[:, offset : offset + width] = jnp.where(first, high, low)
        offset += width
    tile = columns_tile([square], count)
    keep[:, offset:] = tile
    send[:, offset:] = tile


def rope_kernel(head_dim, scale, cosine, sine, *refs):
    parts, (out, squares) = refs[:-2], refs[-2:]
    total = parts[0][...]
    for part in parts[1:]:
        total = total + part[...]
    blocks = (total.shape[1] - LANES) // head_dim
    tile = total[:, blocks * head_dim :]
    squares[...] = tile
    row_scale = lax.rsqrt(tile[:, :1] / D + EPS)
    cosines, sines = cosine[...], sine[...]
    for block in range(blocks):
        entry = total[:, block * head_dim : (block + 1) * head_dim] * row_scale
        if block < blocks * 3 // 4:
            entry = entry * cosines + pltpu.roll(entry, head_dim // 2, 1) * sines
        if block < blocks // 2:
            entry = entry * scale
        out[:, block * head_dim : (block + 1) * head_dim] = entry.astype(BF)


def attend_kernel(
    meta, lengths, owners, mine, other, ck, cv, uk, uv, keep, send, queries, numer, denom
):
    slot = pl.program_id(0)
    count, heads, wide = queries.shape
    head_dim = numer.shape[2]
    half = count // 2
    group = half // 2
    half_heads = heads // 2
    half_kv = half_heads // 2
    first = meta[0] == 0
    block_index = meta[1]

    def piece(index, at):
        a = mine[:, at * head_dim : (at + 1) * head_dim].astype(F32)
        b = other[:, at * head_dim : (at + 1) * head_dim].astype(F32)
        return jnp.where(first, a, b) if index == 0 else jnp.where(first, b, a)

    @pl.when(slot == 0)
    def _():
        queries[...] = jnp.zeros_like(queries)
        for head in range(heads):
            kv = head // 2
            queries[:, head, kv * head_dim : (kv + 1) * head_dim] = piece(
                head // half_heads, head % half_heads
            )

    head_row = lax.broadcasted_iota(jnp.int32, (heads, head_dim), 0)
    for kind, (key_ref, value_ref) in enumerate(((ck, cv), (uk, uv))):
        block_len = key_ref.shape[1]
        request = owners[kind, slot]
        length = lengths[kind, request]
        row = request // group * half + kind * group + request % group
        query = queries[row].astype(BF)
        scores = nt_dot(query, key_ref[0])
        place = block_index * block_len + lax.broadcasted_iota(jnp.int32, scores.shape, 1)
        probs = jnp.where(
            place < length, jnp.exp(ATTN_CAP * jnp.tanh(scores / ATTN_CAP)), 0.0
        )
        sums = nn_dot(probs.astype(BF), value_ref[0])
        folded = jnp.zeros((heads, head_dim), F32)
        for kv in range(heads // 2):
            folded = jnp.where(
                head_row // 2 == kv, sums[:, kv * head_dim : (kv + 1) * head_dim], folded
            )
        numer[row] = folded
        denom[row] = jnp.broadcast_to(
            jnp.sum(probs, axis=-1, keepdims=True), (heads, head_dim)
        )

    @pl.when(slot == pl.num_programs(0) - 1)
    def _():
        owned = jnp.where(block_index == 0, 1.0, 0.0)
        sums, totals = [], []
        for head in range(heads):
            side = head // half_heads
            kv = head % half_heads // 2
            query = piece(side, head % half_heads)
            key = piece(side, half_heads + kv)
            value = piece(side, half_heads + half_kv + kv)
            score = jnp.sum(query * key, axis=-1, keepdims=True)
            own = jnp.exp(ATTN_CAP * jnp.tanh(score / ATTN_CAP))
            weight = own.astype(BF).astype(F32)
            sums.append(numer[:, head, :] + owned * weight * value)
            totals.append(denom[:, head, :1] + owned * own)
        for at in range(half_heads):
            low, high = sums[at], sums[half_heads + at]
            keep[:, at * head_dim : (at + 1) * head_dim] = jnp.where(first, low, high)
            send[:, at * head_dim : (at + 1) * head_dim] = jnp.where(first, high, low)
        low = columns_tile(totals[:half_heads], count)
        high = columns_tile(totals[half_heads:], count)
        keep[:, half_heads * head_dim :] = jnp.where(first, low, high)
        send[:, half_heads * head_dim :] = jnp.where(first, high, low)


def attended_kernel(*refs):
    parts, out = refs[:-1], refs[-1]
    total = parts[0][...]
    for part in parts[1:]:
        total = total + part[...]
    width = out.shape[1]
    heads = width // HD
    for head in range(heads):
        at = slice(head * HD, (head + 1) * HD)
        out[:, at] = (total[:, at] / total[:, width + head : width + head + 1]).astype(BF)


def output_kernel(meta, mine, other, weight, out):
    first = meta[0] == 0
    a, b = mine[...].astype(F32), other[...].astype(F32)
    low = jnp.where(first, a, b).astype(BF)
    high = jnp.where(first, b, a).astype(BF)
    width = mine.shape[1]
    out[...] = nt_dot(low, weight[:, :width]) + nt_dot(high, weight[:, width:])


def gate_up_kernel(pieces, meta, hidden, post_gain, pre_gain, *refs):
    parts, (gate_weight, up_weight, keep, send, branch, inputs, tile) = refs[:-7], refs[-7:]
    step = pl.program_id(0)
    count = hidden.shape[0]
    guide, place = meta[0], meta[2]

    @pl.when(step == 0)
    def _():
        projected = parts[0][...]
        for part in parts[1:]:
            projected = projected + part[...]
        streams = hidden[...].astype(F32)
        gained = projected * post_gain[...]
        branch[...] = gained
        inputs[:count, :] = (streams * pre_gain[...]).astype(BF)
        inputs[count:, :] = (gained * pre_gain[...]).astype(BF)
        tile[...] = columns_tile(
            [
                jnp.sum(projected * projected, axis=-1, keepdims=True),
                jnp.sum(streams * gained, axis=-1, keepdims=True),
                jnp.sum(gained * gained, axis=-1, keepdims=True),
            ],
            count,
        )

    operand = inputs[...]
    gate = nn_dot(operand, gate_weight[...])
    up = nn_dot(operand, up_weight[...])
    width = gate.shape[1]
    slot = lax.bitwise_xor(lax.rem(step, pieces), place)
    mine = lax.div(step, pieces) == guide

    @pl.when(mine)
    def _():
        keep[slot, :, :width] = gate
        keep[slot, :, width : 2 * width] = up
        keep[slot, :count, 2 * width :] = tile[...]
        keep[slot, count:, 2 * width :] = jnp.zeros((count, LANES), F32)

    @pl.when(jnp.logical_not(mine))
    def _():
        send[slot, :, :width] = gate.astype(BF)
        send[slot, :, width : 2 * width] = up.astype(BF)
        coded = split_tile(tile[...])
        send[slot, :count, 2 * width :] = coded
        send[slot, count:, 2 * width :] = jnp.zeros_like(coded)


def share_kernel(keep, got, own, *outs):
    width = keep.shape[2] - LANES
    count = keep.shape[1] // 2
    tile = keep[0, :count, width:] + joined_tile(got[0, :count, width:])
    own[:, :width] = keep[0, :, :width] + got[0, :, :width].astype(F32)
    own[:count, width:] = tile
    own[count:, width:] = jnp.zeros((count, LANES), F32)
    coded = split_tile(tile)
    for at, out in enumerate(outs):
        out[:, :width] = (
            keep[at + 1, :, :width] + got[at + 1, :, :width].astype(F32)
        ).astype(BF)
        out[:count, width:] = coded
        out[count:, width:] = jnp.zeros_like(coded)


def active_kernel(squares, own, *refs):
    parts, (out, scales) = refs[:-2], refs[-2:]
    count = squares.shape[0]
    width = out.shape[1]
    tile = own[:count, 2 * width :]
    for part in parts:
        tile = tile + joined_tile(part[:count, 2 * width :])
    branch_scale = lax.rsqrt(tile[:, 0:1] / D + EPS)
    middle_sq = squares[:, 0:1] + branch_scale * (
        2.0 * tile[:, 1:2] + branch_scale * tile[:, 2:3]
    )
    scale = lax.rsqrt(jnp.maximum(middle_sq, 0.0) / D + EPS)
    scales[...] = jnp.broadcast_to(branch_scale, (count, LANES))

    def summed(rows, at):
        total = own[rows, at]
        for part in parts:
            total = total + part[rows, at].astype(F32)
        return total

    low, high = slice(0, count), slice(count, 2 * count)
    gate_at, up_at = slice(0, width), slice(width, 2 * width)
    gate = (summed(low, gate_at) + branch_scale * summed(high, gate_at)) * scale
    up = (summed(low, up_at) + branch_scale * summed(high, up_at)) * scale
    out[...] = (jax.nn.gelu(gate, approximate=True) * up).astype(BF)


def down_kernel(pieces, meta, *refs):
    mine, other = refs[:pieces], refs[pieces : 2 * pieces]
    weight, out = refs[2 * pieces :]
    step = pl.program_id(0)

    @pl.when(step == 0)
    def _():
        out[...] = jnp.zeros_like(out)

    for at, part in enumerate(mine + other):

        @pl.when(step == at)
        def _(part=part):
            out[...] += nt_dot(part[...], weight[...])


def last_kernel(hidden, branch, scales, post_gain, final_gain, *refs):
    parts, out = refs[:-1], refs[-1]
    ffw = parts[0][...]
    for part in parts[1:]:
        ffw = ffw + part[...]
    count = ffw.shape[0]
    middle = hidden[...].astype(F32) + branch[...] * scales[:, 0:1]
    gained = ffw * post_gain[...]
    out[:count, :] = (middle * final_gain[...]).astype(BF)
    out[count : 2 * count, :] = (gained * final_gain[...]).astype(BF)
    tile = columns_tile(
        [
            jnp.sum(ffw * ffw, axis=-1, keepdims=True),
            jnp.sum(middle * gained, axis=-1, keepdims=True),
            jnp.sum(gained * gained, axis=-1, keepdims=True),
            jnp.sum(middle * middle, axis=-1, keepdims=True),
        ],
        count,
    )
    out[2 * count :, :LANES] = split_tile(tile)
    out[2 * count :, LANES:] = jnp.zeros((count, out.shape[1] - LANES), BF)


def table_kernel(pieces, meta, *refs):
    parts, (table, keep, send, rows) = refs[:pieces], refs[pieces:]
    step = pl.program_id(0)
    count = parts[0].shape[0] // 3
    half = count // 2
    width = parts[0].shape[1]
    first = meta[0] == 0
    place = meta[2]
    step_rows = table.shape[0]
    total_rows = keep.shape[1] - LANES

    @pl.when(step == 0)
    def _():
        for target in range(pieces):
            block = parts[0][: 2 * count, :].astype(F32)
            for at in range(1, pieces):
                block = jnp.where(
                    lax.bitwise_xor(place, at) == target,
                    parts[at][: 2 * count, :].astype(F32),
                    block,
                )
            rows[:, target * width : (target + 1) * width] = block
        tile = joined_tile(parts[0][2 * count :, :LANES])
        for at in range(1, pieces):
            tile = tile + joined_tile(parts[at][2 * count :, :LANES])
        low, high = tile[:half], tile[half:]
        keep[:half, total_rows:] = jnp.where(first, low, high)
        send[:half, total_rows:] = jnp.where(first, high, low)
        keep[half:, total_rows:] = jnp.zeros((half, LANES), F32)
        send[half:, total_rows:] = jnp.zeros((half, LANES), F32)

    product = nt_dot(rows[...].astype(BF), table[...])
    at = pl.ds(pl.multiple_of(step * step_rows, step_rows), step_rows)
    for base in (0, half):
        low = product[2 * base : 2 * base + half]
        high = product[2 * base + half : 2 * base + 2 * half]
        keep[base : base + half, at] = jnp.where(first, low, high)
        send[base : base + half, at] = jnp.where(first, high, low)


def logits_kernel(places, weights, keep, got, out, mixed):
    rows = keep.shape[0] // 2
    group = rows // 2
    total_rows = keep.shape[1] - LANES
    tile = keep[:rows, total_rows:] + got[:rows, total_rows:]
    branch_scale = lax.rsqrt(tile[:, 0:1] / D + EPS)
    last_sq = tile[:, 3:4] + branch_scale * (
        2.0 * tile[:, 1:2] + branch_scale * tile[:, 2:3]
    )
    scale = lax.rsqrt(jnp.maximum(last_sq, 0.0) / D + EPS)
    sums = keep[:, :total_rows] + got[:, :total_rows]
    logits = LOGIT_CAP * jnp.tanh(
        (sums[:rows] + branch_scale * sums[rows:]) * scale / LOGIT_CAP
    )
    turned = pltpu.roll(logits, group, 0)
    top = lax.broadcasted_iota(jnp.int32, logits.shape, 0) < group
    uncond = jnp.where(top, turned, logits)
    cond = jnp.where(top, logits, turned)
    mixed[...] = uncond + weights[:, 0:1] * (cond - uncond)
    half = places.shape[1]
    for start in range(0, half, LANES):
        at = slice(start, start + LANES)
        wanted = places[:, at]
        lane = lax.bitwise_and(wanted, LANES - 1)
        chunk = lax.shift_right_logical(wanted, 7)
        found = jnp.zeros((rows, LANES), F32)
        for block in range(total_rows // LANES):
            values = mixed[:, block * LANES : (block + 1) * LANES]
            found = jnp.where(
                chunk == block, jnp.take_along_axis(values, lane, axis=1), found
            )
        out[:, start : start + LANES] = found[:group]
        out[:, half + start : half + start + LANES] = found[group:]


def from_peers(value, axis, size):
    values = value if isinstance(value, (list, tuple)) else [value] * (size - 1)
    return [
        lax.ppermute(values[k - 1], axis, [(i, i ^ k) for i in range(size)])
        for k in range(1, size)
    ]


def fast_layer(
    hidden,
    lengths,
    slot_owner,
    allowed_ids,
    guidance,
    pre_attn_gain,
    post_attn_gain,
    pre_ffw_gain,
    post_ffw_gain,
    final_gain,
    query_weight,
    key_weight,
    value_weight,
    output_weight,
    gate_weight,
    up_weight,
    down_weight,
    embedding,
    cond_keys,
    cond_values,
    uncond_keys,
    uncond_values,
):
    kinds, requests, width = hidden.shape
    count = kinds * requests
    half = count // 2
    group = half // 2
    heads = query_weight.shape[1] // HD
    kv_heads = key_weight.shape[1] // HD
    seq_size = lax.axis_size("seq")
    kv_size = lax.axis_size("kv")
    guide_index = lax.axis_index("guide")
    seq_index = lax.axis_index("seq")
    kv_index = lax.axis_index("kv")
    meta = jnp.stack([guide_index, guide_index * seq_size + seq_index, seq_index]).astype(jnp.int32)
    shape = jax.ShapeDtypeStruct
    row = lambda gain: gain.reshape(1, -1)

    position = (
        lengths.astype(F32).reshape(kinds, 2, group).transpose(1, 0, 2).reshape(count)
    )
    half_dim = HD // 2
    frequency = THETA ** (-2.0 * jnp.arange(half_dim, dtype=F32) / HD)
    angles = position[:, None] * frequency
    cosine = jnp.cos(angles)
    sine = jnp.sin(angles)
    cosine = jnp.concatenate([cosine, cosine], axis=-1)
    sine = jnp.concatenate([-sine, sine], axis=-1)

    with jax.named_scope("project"):
        joint = (heads + 2 * kv_heads) * HD // 2 + LANES
        rows, keep, send = pl.pallas_call(
            project_kernel,
            out_shape=(
                shape((count, width), BF),
                shape((count, joint), F32),
                shape((count, joint), F32),
            ),
            in_specs=[SMEM] + [VMEM] * 5,
            out_specs=(VMEM,) * 3,
            compiler_params=limit(16),
        )(meta, hidden.reshape(count, width), row(pre_attn_gain), query_weight, key_weight, value_weight)
        total = keep + from_peers(send, "guide", 2)[0]
        parts = [total] + from_peers(total, "seq", seq_size)
        mine, squares = pl.pallas_call(
            lambda *refs: rope_kernel(HD, (D // H) ** (-0.5), *refs),
            out_shape=(shape((count, joint - LANES), BF), shape((count, LANES), F32)),
            in_specs=[VMEM] * (2 + seq_size),
            out_specs=(VMEM,) * 2,
            compiler_params=limit(16),
        )(cosine, sine, *parts)
        other = from_peers(mine, "guide", 2)[0]

    with jax.named_scope("attend"):
        cond_len, uncond_len = cond_keys.shape[1], uncond_keys.shape[1]
        kv_width = kv_heads * HD
        block = lambda size: pl.BlockSpec((1, size, kv_width), lambda i, *_: (i, 0, 0))
        whole = pl.BlockSpec((count, joint - LANES), lambda i, *_: (0, 0))
        attend_width = heads // 2 * HD + LANES
        out_block = pl.BlockSpec((count, attend_width), lambda i, *_: (0, 0))
        keep, send = pl.pallas_call(
            attend_kernel,
            out_shape=(shape((count, attend_width), F32),) * 2,
            grid_spec=pltpu.PrefetchScalarGridSpec(
                num_scalar_prefetch=3,
                grid=(requests,),
                in_specs=[whole, whole] + [block(cond_len)] * 2 + [block(uncond_len)] * 2,
                out_specs=(out_block,) * 2,
                scratch_shapes=[
                    pltpu.VMEM((count, heads, kv_width), F32),
                    pltpu.VMEM((count, heads, HD), F32),
                    pltpu.VMEM((count, heads, HD), F32),
                ],
            ),
            compiler_params=limit(24),
        )(meta, lengths, slot_owner, mine, other, cond_keys, cond_values, uncond_keys, uncond_values)
        total = keep + from_peers(send, "guide", 2)[0]
        parts = [total] + from_peers(total, "seq", seq_size)
        mine = pl.pallas_call(
            attended_kernel,
            out_shape=shape((count, heads // 2 * HD), BF),
            in_specs=[VMEM] * seq_size,
            out_specs=VMEM,
            compiler_params=limit(16),
        )(*parts)
        other = from_peers(mine, "guide", 2)[0]
        part = pl.pallas_call(
            output_kernel,
            out_shape=shape((count, width), F32),
            in_specs=[SMEM] + [VMEM] * 3,
            out_specs=VMEM,
            compiler_params=limit(16),
        )(meta, mine, other, output_weight.T)
        parts = [part] + from_peers(part, "kv", kv_size)

    with jax.named_scope("gate_up"):
        hidden_units = gate_weight.shape[1]
        unit_block = hidden_units // (2 * seq_size)
        share_width = 2 * unit_block + LANES
        const2 = lambda i, *_: (0, 0)
        small = pl.BlockSpec((count, width), const2)
        gain_block = pl.BlockSpec((1, width), const2)
        weight_block = pl.BlockSpec((width, unit_block), lambda i, *_: (0, i))
        share_block = pl.BlockSpec((seq_size, 2 * count, share_width), lambda i, *_: (0, 0, 0))
        keep, send, branch = pl.pallas_call(
            lambda *refs: gate_up_kernel(seq_size, *refs),
            out_shape=(
                shape((seq_size, 2 * count, share_width), F32),
                shape((seq_size, 2 * count, share_width), BF),
                shape((count, width), F32),
            ),
            grid_spec=pltpu.PrefetchScalarGridSpec(
                num_scalar_prefetch=1,
                grid=(2 * seq_size,),
                in_specs=[small, gain_block, gain_block] + [small] * kv_size + [weight_block] * 2,
                out_specs=(share_block, share_block, small),
                scratch_shapes=[
                    pltpu.VMEM((2 * count, width), BF),
                    pltpu.VMEM((count, LANES), F32),
                ],
            ),
            compiler_params=limit(24),
        )(meta, rows, row(post_attn_gain), row(pre_ffw_gain), *parts, gate_weight, up_weight)
        got = from_peers(send, "guide", 2)[0]
        own, *shares = pl.pallas_call(
            share_kernel,
            out_shape=(shape((2 * count, share_width), F32),)
            + (shape((2 * count, share_width), BF),) * (seq_size - 1),
            in_specs=[VMEM] * 2,
            out_specs=(VMEM,) * seq_size,
            compiler_params=limit(16),
        )(keep, got)
        parts = from_peers(shares, "seq", seq_size)
        active, scales = pl.pallas_call(
            active_kernel,
            out_shape=(shape((count, unit_block), BF), shape((count, LANES), F32)),
            in_specs=[VMEM] * (1 + seq_size),
            out_specs=(VMEM,) * 2,
            compiler_params=limit(16),
        )(squares, own, *parts)

    with jax.named_scope("down"):
        mine = [active] + from_peers(active, "seq", seq_size)
        other = [from_peers(value, "guide", 2)[0] for value in mine]

        def weight_place(i, meta_ref):
            side = jnp.where(i < seq_size, meta_ref[0], 1 - meta_ref[0])
            return (0, side * seq_size + lax.bitwise_xor(lax.rem(i, seq_size), meta_ref[2]))

        part = pl.pallas_call(
            lambda *refs: down_kernel(seq_size, *refs),
            out_shape=shape((count, width), F32),
            grid_spec=pltpu.PrefetchScalarGridSpec(
                num_scalar_prefetch=1,
                grid=(2 * seq_size,),
                in_specs=[pl.BlockSpec((count, unit_block), const2)] * (2 * seq_size)
                + [pl.BlockSpec((width, unit_block), weight_place)],
                out_specs=small,
            ),
            compiler_params=limit(16),
        )(meta, *mine, *other, down_weight.T)
        parts = [part] + from_peers(part, "kv", kv_size)

    with jax.named_scope("head"):
        mine = pl.pallas_call(
            last_kernel,
            out_shape=shape((3 * count, width), BF),
            in_specs=[VMEM] * (5 + kv_size),
            out_specs=VMEM,
            compiler_params=limit(16),
        )(rows, branch, scales, row(post_ffw_gain), row(final_gain), *parts)
        parts = [mine] + from_peers(mine, "seq", seq_size)
        table_rows, table_width = embedding.shape
        step_rows = min(512, table_rows)
        piece_block = pl.BlockSpec((3 * count, width), const2)
        logit_block = pl.BlockSpec((count, table_rows + LANES), const2)
        keep, send = pl.pallas_call(
            lambda *refs: table_kernel(seq_size, *refs),
            out_shape=(shape((count, table_rows + LANES), F32),) * 2,
            grid_spec=pltpu.PrefetchScalarGridSpec(
                num_scalar_prefetch=1,
                grid=(table_rows // step_rows,),
                in_specs=[piece_block] * seq_size
                + [pl.BlockSpec((step_rows, table_width), lambda i, *_: (i, 0))],
                out_specs=(logit_block,) * 2,
                scratch_shapes=[pltpu.VMEM((2 * count, table_width), F32)],
            ),
            compiler_params=limit(24),
        )(meta, *parts, embedding)
        got = from_peers(send, "guide", 2)[0]
        allowed = allowed_ids.shape[0]
        places = allowed_ids - (kv_index * seq_size + seq_index) * table_rows
        places = jnp.repeat(places.reshape(2, allowed // 2), group, axis=0)
        weights = lax.dynamic_slice_in_dim(guidance, guide_index * group, group, 0)
        weights = jnp.broadcast_to(jnp.concatenate([weights, weights])[:, None], (half, LANES))
        return pl.pallas_call(
            logits_kernel,
            out_shape=shape((group, allowed), F32),
            in_specs=[VMEM] * 4,
            out_specs=VMEM,
            scratch_shapes=[pltpu.VMEM((half, table_rows), F32)],
            compiler_params=limit(24),
        )(places, weights, keep, got)


def on_device(*arrays):
    units = arrays[14].shape[1] // (2 * lax.axis_size("seq"))
    requests = arrays[0].shape[1]
    if units % LANES or requests != 8 or lax.axis_size("guide") != 2:
        return plain_layer(*arrays)
    return fast_layer(*arrays)


def solution(mesh):
    return jax.shard_map(
        on_device,
        mesh=mesh,
        in_specs=(
            P(None, None, ("guide", "seq")),
            P(),
            P(),
            P(("kv", "seq")),
            P(),
            P(("guide", "seq")),
            P(("guide", "seq")),
            P(("guide", "seq")),
            P(("guide", "seq")),
            P(("guide", "seq")),
            P(("guide", "seq"), "kv"),
            P(("guide", "seq"), "kv"),
            P(("guide", "seq"), "kv"),
            P("kv", ("guide", "seq")),
            P(("guide", "seq"), "kv"),
            P(("guide", "seq"), "kv"),
            P("kv", ("guide", "seq")),
            P(("kv", "seq"), "guide"),
            P(None, ("guide", "seq"), "kv"),
            P(None, ("guide", "seq"), "kv"),
            P(None, ("guide", "seq"), "kv"),
            P(None, ("guide", "seq"), "kv"),
        ),
        out_specs=P("guide", ("kv", "seq")),
        check_vma=False,
    )
```

```python
import jax
import jax.numpy as jnp
from jax import lax
from jax.experimental import pallas as pl
from jax.experimental.pallas import tpu as pltpu
from jax.sharding import PartitionSpec as P

D = 4608
H = 32
HD = 128


EPS = 1e-06
ATTN_CAP = 50.0
LOGIT_CAP = 30.0
THETA = 10000.0
HIGHEST = lax.Precision.HIGHEST


def rotary(values, position):
    half_size = values.shape[-1] // 2
    frequency = THETA ** (-2.0 * jnp.arange(half_size, dtype=jnp.float32) / values.shape[-1])
    angles = position[:, None, None] * frequency
    first_half = values[..., :half_size]
    second_half = values[..., half_size:]
    cosine = jnp.cos(angles)
    sine_part = jnp.sin(angles)
    return jnp.concatenate(
        [
            first_half * cosine - second_half * sine_part,
            second_half * cosine + first_half * sine_part,
        ],
        axis=-1,
    )


def to_slots(slot_pick, array):
    flat = array.astype(jnp.float32).reshape(array.shape[0], array.shape[1], -1)
    moved = jnp.einsum("gsr,gre->gse", slot_pick, flat, precision=HIGHEST)
    return moved.reshape(array.shape).astype(array.dtype)


def to_requests(slot_pick, array):
    flat = array.astype(jnp.float32).reshape(array.shape[0], array.shape[1], -1)
    moved = jnp.einsum("gsr,gse->gre", slot_pick, flat, precision=HIGHEST)
    return moved.reshape(array.shape).astype(array.dtype)


def attend_block(queries, key_block, value_block, slot_len, first_pos, tile_len):
    slot_count, block_len = (key_block.shape[0], key_block.shape[1])
    local_kv, group_size, head_size = (queries.shape[1], queries.shape[2], queries.shape[3])
    live_len = jnp.clip(jnp.max(slot_len) - first_pos, 0, block_len)
    tile_count = (live_len + tile_len - 1) // tile_len

    def one_tile(tile_index, carry):
        numer, denom = carry
        tile_start = tile_index * tile_len
        key_tile = lax.dynamic_slice_in_dim(key_block, tile_start, tile_len, 1).reshape(
            slot_count, tile_len, local_kv, head_size
        )
        value_tile = lax.dynamic_slice_in_dim(value_block, tile_start, tile_len, 1).reshape(
            slot_count, tile_len, local_kv, head_size
        )
        scores = jnp.einsum(
            "rkgd,rtkd->rkgt", queries, key_tile, preferred_element_type=jnp.float32
        )
        places = first_pos + tile_start + jnp.arange(tile_len, dtype=jnp.int32)
        visible = places[None, None, None, :] < slot_len[:, None, None, None]
        probs = jnp.where(visible, jnp.exp(ATTN_CAP * jnp.tanh(scores / ATTN_CAP)), 0.0)
        numer = numer + jnp.einsum(
            "rkgt,rtkd->rkgd",
            probs.astype(jnp.bfloat16),
            value_tile,
            preferred_element_type=jnp.float32,
        )
        denom = denom + jnp.sum(probs, axis=-1)
        return (numer, denom)

    start_numer = jnp.zeros((slot_count, local_kv, group_size, head_size), jnp.float32)
    start_denom = jnp.zeros((slot_count, local_kv, group_size), jnp.float32)
    return lax.fori_loop(0, tile_count, one_tile, (start_numer, start_denom))


def plain_layer(
    hidden,
    lengths,
    slot_owner,
    allowed_ids,
    guidance,
    pre_attn_gain,
    post_attn_gain,
    pre_ffw_gain,
    post_ffw_gain,
    final_gain,
    query_weight,
    key_weight,
    value_weight,
    output_weight,
    gate_weight,
    up_weight,
    down_weight,
    embedding,
    cond_keys,
    cond_values,
    uncond_keys,
    uncond_values,
):
    kinds, requests, width_local = hidden.shape
    stream_count = kinds * requests
    local_heads = query_weight.shape[1] // HD
    local_kv = key_weight.shape[1] // HD
    group_size = local_heads // local_kv
    streams = hidden.astype(jnp.float32)
    normed = (streams * pre_attn_gain).astype(jnp.bfloat16).reshape(stream_count, width_local)
    query_part = jnp.dot(normed, query_weight, preferred_element_type=jnp.float32)
    key_part = jnp.dot(normed, key_weight, preferred_element_type=jnp.float32)
    value_part = jnp.dot(normed, value_weight, preferred_element_type=jnp.float32)
    square_part = jnp.sum(streams * streams, axis=-1)
    square_sum, query_sum, key_sum, value_sum = lax.psum(
        (square_part, query_part, key_part, value_part), ("guide", "seq")
    )
    row_scale = lax.rsqrt(square_sum / D + EPS).reshape(stream_count, 1)
    position = lengths.astype(jnp.float32).reshape(stream_count)
    queries = (
        rotary((query_sum * row_scale).reshape(stream_count, local_heads, HD), position)
        * (D // H) ** (-0.5)
    ).astype(jnp.bfloat16)
    new_keys = rotary((key_sum * row_scale).reshape(stream_count, local_kv, HD), position).astype(
        jnp.bfloat16
    )
    new_values = (value_sum * row_scale).astype(jnp.bfloat16)
    queries = queries.reshape(kinds, requests, local_kv, group_size, HD)
    new_keys = new_keys.reshape(kinds, requests, local_kv, HD)
    new_values = new_values.reshape(kinds, requests, local_kv, HD)
    matches = slot_owner[:, :, None] == jnp.arange(requests, dtype=jnp.int32)[None, None, :]
    slot_pick = matches.astype(jnp.float32)
    slot_len = jnp.sum(jnp.where(matches, lengths[:, None, :], 0), axis=-1)
    slot_queries = to_slots(slot_pick, queries)
    slot_keys = to_slots(slot_pick, new_keys)
    slot_values = to_slots(slot_pick, new_values)
    guide_index = lax.axis_index("guide")
    seq_index = lax.axis_index("seq")
    block_index = guide_index * lax.axis_size("seq") + seq_index
    cond_len = cond_keys.shape[1]
    uncond_len = uncond_keys.shape[1]
    cond_numer, cond_denom = attend_block(
        slot_queries[0],
        cond_keys,
        cond_values,
        slot_len[0],
        block_index * cond_len,
        min(256, cond_len),
    )
    uncond_numer, uncond_denom = attend_block(
        slot_queries[1],
        uncond_keys,
        uncond_values,
        slot_len[1],
        block_index * uncond_len,
        min(256, uncond_len),
    )
    numer_part = jnp.stack([cond_numer, uncond_numer])
    denom_part = jnp.stack([cond_denom, uncond_denom])
    numer_sum, denom_sum = lax.psum((numer_part, denom_part), ("guide", "seq"))
    own_score = jnp.einsum(
        "gskjd,gskd->gskj", slot_queries, slot_keys, preferred_element_type=jnp.float32
    )
    own_prob = jnp.exp(ATTN_CAP * jnp.tanh(own_score / ATTN_CAP))
    own_weight = own_prob.astype(jnp.bfloat16).astype(jnp.float32)
    numer_total = (
        numer_sum + own_weight[..., None] * slot_values.astype(jnp.float32)[:, :, :, None, :]
    )
    denom_total = denom_sum + own_prob
    attended_slots = (numer_total / denom_total[..., None]).astype(jnp.bfloat16)
    attended = to_requests(slot_pick, attended_slots).reshape(stream_count, local_heads * HD)
    out_part = jnp.dot(attended, output_weight, preferred_element_type=jnp.float32)
    projected = lax.psum(out_part, "kv").reshape(kinds, requests, width_local)
    branch_sq = lax.psum(jnp.sum(projected * projected, axis=-1), ("guide", "seq"))
    out_scale = lax.rsqrt(branch_sq / D + EPS)
    middle = streams + projected * out_scale[..., None] * post_attn_gain
    middle_sq = lax.psum(jnp.sum(middle * middle, axis=-1), ("guide", "seq"))
    ffw_in = (middle * pre_ffw_gain).astype(jnp.bfloat16).reshape(stream_count, width_local)
    ffw_scale = lax.rsqrt(middle_sq / D + EPS).reshape(stream_count, 1)
    gate_part = jnp.dot(ffw_in, gate_weight, preferred_element_type=jnp.float32)
    upward_part = jnp.dot(ffw_in, up_weight, preferred_element_type=jnp.float32)
    gate_sum, upward_sum = lax.psum((gate_part, upward_part), ("guide", "seq"))
    activ = (jax.nn.gelu(gate_sum * ffw_scale, approximate=True) * (upward_sum * ffw_scale)).astype(
        jnp.bfloat16
    )
    down_part = jnp.dot(activ, down_weight, preferred_element_type=jnp.float32)
    ffw_out = lax.psum(down_part, "kv").reshape(kinds, requests, width_local)
    ffw_sq = lax.psum(jnp.sum(ffw_out * ffw_out, axis=-1), ("guide", "seq"))
    branch_scale = lax.rsqrt(ffw_sq / D + EPS)
    last = middle + ffw_out * branch_scale[..., None] * post_ffw_gain
    last_sq = lax.psum(jnp.sum(last * last, axis=-1), ("guide", "seq"))
    final_scale = lax.rsqrt(last_sq / D + EPS)
    final_rows = (last * final_gain).astype(jnp.bfloat16)
    half_rows = lax.all_gather(final_rows, "seq", axis=2, tiled=True)
    table_rows = embedding.shape[0]
    block_first = (lax.axis_index("kv") * lax.axis_size("seq") + seq_index) * table_rows
    picked = jnp.take(embedding, allowed_ids - block_first, axis=0)
    logit_part = jnp.einsum(
        "sd,ad->sa",
        half_rows.reshape(stream_count, half_rows.shape[2]),
        picked,
        preferred_element_type=jnp.float32,
    )
    logit_term = jnp.transpose(logit_part.reshape(kinds, requests, picked.shape[0]), (1, 0, 2))
    logit_share = lax.psum_scatter(logit_term, "guide", scatter_dimension=0, tiled=True)
    half_req = requests // 2
    first_req = guide_index * half_req
    share_scale = jnp.transpose(
        lax.dynamic_slice_in_dim(final_scale, first_req, half_req, 1), (1, 0)
    )
    capped = LOGIT_CAP * jnp.tanh(logit_share * share_scale[:, :, None] / LOGIT_CAP)
    share_weight = lax.dynamic_slice_in_dim(guidance, first_req, half_req, 0)
    return capped[:, 1] + share_weight[:, None] * (capped[:, 0] - capped[:, 1])


BF = jnp.bfloat16
F32 = jnp.float32
LANES = 128
ANY = pl.BlockSpec(memory_space=pl.ANY)
VMEM = pl.BlockSpec(memory_space=pltpu.VMEM)
SMEM = pl.BlockSpec(memory_space=pltpu.SMEM)
MIB = 1 << 20
COPIES = 4


def nt_dot(a, b):
    return lax.dot_general(a, b, (((1,), (1,)), ((), ())), preferred_element_type=F32)


def nn_dot(a, b):
    return jnp.dot(a, b, preferred_element_type=F32)


def in_hbm(value):
    return pltpu.with_memory_space_constraint(value, pltpu.HBM)


def started(sources, targets, done):
    copies = [
        pltpu.make_async_copy(source, target, done.at[at])
        for at, (source, target) in enumerate(zip(sources, targets))
    ]
    for copy in copies:
        copy.start()
    return copies


def limit(mib):
    return pltpu.CompilerParams(vmem_limit_bytes=mib * MIB)


def columns_tile(values, rows):
    lane = lax.broadcasted_iota(jnp.int32, (rows, LANES), 1)
    tile = jnp.zeros((rows, LANES), F32)
    for place, value in enumerate(values):
        tile = jnp.where(lane == place, value, tile)
    return tile


def split_tile(tile):
    high = tile.astype(BF).astype(F32)
    rest = tile - high
    middle = rest.astype(BF).astype(F32)
    low = (rest - middle).astype(BF).astype(F32)
    return (high + pltpu.roll(middle, 32, 1) + pltpu.roll(low, 64, 1)).astype(BF)


def joined_tile(tile):
    terms = tile.astype(F32)
    total = terms + pltpu.roll(terms, LANES - 32, 1) + pltpu.roll(terms, LANES - 64, 1)
    lane = lax.broadcasted_iota(jnp.int32, total.shape, 1)
    return jnp.where(lane < 32, total, 0.0)


def project_kernel(meta, *refs):
    sources, (rows, keep, send), held, done = refs[:5], refs[5:8], refs[8:13], refs[13]
    copies = started(sources, held, done)
    hidden, gain, *weights = held
    for copy in copies[:2]:
        copy.wait()
    count = hidden.shape[0]
    half = count // 2
    group = half // 2
    row = lax.broadcasted_iota(jnp.int32, (count, count), 0)
    column = lax.broadcasted_iota(jnp.int32, (count, count), 1)
    source = (row // group) % 2 * half + row // half * group + row % group
    pick = jnp.where(column == source, 1.0, 0.0).astype(BF)
    streams = nn_dot(pick, hidden[...])
    rows[...] = streams.astype(BF)
    square = jnp.sum(streams * streams, axis=-1, keepdims=True)
    normed = (streams * gain[...].reshape(1, -1)).astype(BF)
    first = meta[0] == 0
    offset = 0
    for copy, weight in zip(copies[2:], weights):
        copy.wait()
        product = nn_dot(normed, weight[...])
        width = product.shape[1] // 2
        low, high = product[:, :width], product[:, width:]
        keep[:, offset : offset + width] = jnp.where(first, low, high)
        send[:, offset : offset + width] = jnp.where(first, high, low)
        offset += width
    tile = columns_tile([square], count)
    keep[:, offset:] = tile
    send[:, offset:] = tile


def hold_kernel(starts, *refs):
    count = len(starts)
    sources, (*targets, token, done) = refs[1 : count + 1], refs[count + 1 :]
    token[...] = jnp.zeros_like(token)
    pieces = []
    for start, source, target in zip(starts, sources, targets):
        size = target.shape[0] // COPIES
        pieces += [
            (source.at[pl.ds(start + at * size, size)], target.at[pl.ds(at * size, size)])
            for at in range(COPIES)
        ]
    for copy in started(*zip(*pieces), done):
        copy.wait()


def held_near(after, *values):
    arrays = [array for array, _, _ in values]
    starts = [start for _, start, _ in values]
    shapes = [(rows,) + array.shape[1:] for array, _, rows in values]
    size = sum(rows * array.shape[-1] * 2 for array, _, rows in values)
    return pl.pallas_call(
        lambda *refs: hold_kernel(starts, *refs),
        out_shape=[pltpu.VMEM(held, array.dtype) for held, array in zip(shapes, arrays)]
        + [jax.ShapeDtypeStruct((8, LANES), F32)],
        in_specs=[ANY] * (1 + len(values)),
        out_specs=[VMEM] * (1 + len(values)),
        scratch_shapes=[pltpu.SemaphoreType.DMA((COPIES * len(values),))],
        cost_estimate=pl.CostEstimate(flops=0, bytes_accessed=2 * size, transcendentals=0),
        compiler_params=limit(2),
    )(after, *map(in_hbm, arrays))


def pair_kernel(keep, got, own, coded):
    total = keep[...] + got[...]
    own[...] = total
    width = total.shape[1] - LANES
    coded[:, :width] = total[:, :width].astype(BF)
    coded[:, width:] = split_tile(total[:, width:])


def added_parts(own, parts):
    width = own.shape[1] - LANES
    total, tile = own[:, :width], own[:, width:]
    for part in parts:
        total = total + part[:, :width].astype(F32)
        tile = tile + joined_tile(part[:, width:])
    return total, tile


def rope_kernel(head_dim, scale, cosine, sine, *refs):
    parts, (out, squares) = refs[:-2], refs[-2:]
    total, tile = added_parts(parts[0], parts[1:])
    blocks = total.shape[1] // head_dim
    squares[...] = tile
    row_scale = lax.rsqrt(tile[:, :1] / D + EPS)
    cosines, sines = cosine[...], sine[...]
    for block in range(blocks):
        entry = total[:, block * head_dim : (block + 1) * head_dim] * row_scale
        if block < blocks * 3 // 4:
            entry = entry * cosines + pltpu.roll(entry, head_dim // 2, 1) * sines
        if block < blocks // 2:
            entry = entry * scale
        out[:, block * head_dim : (block + 1) * head_dim] = entry.astype(BF)


def attend_kernel(meta, mine, other, *refs):
    sources, (keep, send), held = refs[:4], refs[4:6], refs[6:10]
    queries, numer, denom, done = refs[10:]
    slots = sources[0].shape[0]
    order = [(slot, which) for slot in range(slots) for which in (0, 2, 1, 3)]
    copies = started(
        [sources[which].at[slot] for slot, which in order],
        [held[which].at[slot] for slot, which in order],
        done,
    )
    arrived = dict(zip(order, copies))
    count, heads, wide = queries.shape
    head_dim = numer.shape[2]
    half = count // 2
    group = half // 2
    half_heads = heads // 2
    half_kv = half_heads // 2
    first = meta[0] == 0
    block_index = meta[1]

    def piece(index, at):
        a = mine[:, at * head_dim : (at + 1) * head_dim].astype(F32)
        b = other[:, at * head_dim : (at + 1) * head_dim].astype(F32)
        return jnp.where(first, a, b) if index == 0 else jnp.where(first, b, a)

    queries[...] = jnp.zeros_like(queries)
    for head in range(heads):
        kv = head // 2
        queries[:, head, kv * head_dim : (kv + 1) * head_dim] = piece(
            head // half_heads, head % half_heads
        )

    def place_of(kind, slot):
        request = meta[3 + (2 + kind) * half + slot]
        row = request // group * half + kind * group + request % group
        return row, meta[3 + kind * half + request]

    def scores_of(kind, slot):
        row, length = place_of(kind, slot)
        query = queries[row].astype(BF)
        scores = nt_dot(query, held[2 * kind][slot])
        place = block_index * scores.shape[1] + lax.broadcasted_iota(jnp.int32, scores.shape, 1)
        return jnp.where(
            place < length, jnp.exp(ATTN_CAP * jnp.tanh(scores / ATTN_CAP)), 0.0
        )

    head_row = lax.broadcasted_iota(jnp.int32, (heads, head_dim), 0)

    def weigh(kind, slot, probs):
        row, _ = place_of(kind, slot)
        sums = nn_dot(probs.astype(BF), held[2 * kind + 1][slot])
        folded = jnp.zeros((heads, head_dim), F32)
        for kv in range(heads // 2):
            folded = jnp.where(
                head_row // 2 == kv, sums[:, kv * head_dim : (kv + 1) * head_dim], folded
            )
        numer[row] = folded
        denom[row] = jnp.broadcast_to(
            jnp.sum(probs, axis=-1, keepdims=True), (heads, head_dim)
        )

    ready = None
    for slot in range(slots + 1):
        if slot < slots:
            arrived[slot, 0].wait()
            arrived[slot, 2].wait()
        if slot > 0:
            arrived[slot - 1, 1].wait()
            arrived[slot - 1, 3].wait()
        following = [scores_of(kind, slot) for kind in (0, 1)] if slot < slots else None
        if ready is not None:
            for kind in (0, 1):
                weigh(kind, slot - 1, ready[kind])
        ready = following

    owned = jnp.where(block_index == 0, 1.0, 0.0)
    sums, totals = [], []
    for head in range(heads):
        side = head // half_heads
        kv = head % half_heads // 2
        query = piece(side, head % half_heads)
        key = piece(side, half_heads + kv)
        value = piece(side, half_heads + half_kv + kv)
        score = jnp.sum(query * key, axis=-1, keepdims=True)
        own = jnp.exp(ATTN_CAP * jnp.tanh(score / ATTN_CAP))
        weight = own.astype(BF).astype(F32)
        sums.append(numer[:, head, :] + owned * weight * value)
        totals.append(denom[:, head, :1] + owned * own)
    for at in range(half_heads):
        low, high = sums[at], sums[half_heads + at]
        keep[:, at * head_dim : (at + 1) * head_dim] = jnp.where(first, low, high)
        send[:, at * head_dim : (at + 1) * head_dim] = jnp.where(first, high, low)
    low = columns_tile(totals[:half_heads], count)
    high = columns_tile(totals[half_heads:], count)
    keep[:, half_heads * head_dim :] = jnp.where(first, low, high)
    send[:, half_heads * head_dim :] = jnp.where(first, high, low)


def attended_kernel(*refs):
    parts, out = refs[:-1], refs[-1]
    total, tile = added_parts(parts[0], parts[1:])
    for head in range(out.shape[1] // HD):
        at = slice(head * HD, (head + 1) * HD)
        out[:, at] = (total[:, at] / tile[:, head : head + 1]).astype(BF)


def output_kernel(meta, mine, other, weight, out):
    first = meta[0] == 0
    a, b = mine[...].astype(F32), other[...].astype(F32)
    low = jnp.where(first, a, b).astype(BF)
    high = jnp.where(first, b, a).astype(BF)
    width = mine.shape[1]
    out[...] = nt_dot(low, weight[:, :width]) + nt_dot(high, weight[:, width:])


def gate_up_kernel(pieces, meta, hidden, post_gain, pre_gain, *refs):
    parts, (gate_weight, up_weight, keep, send, branch, ups, done) = refs[:-7], refs[-7:]
    count = hidden.shape[0]
    width = ups.shape[2]
    guide, place = meta[0], meta[2]
    blocks = [pl.ds(step * width, width) for step in range(2 * pieces)]
    copies = started(
        [up_weight.at[:, block] for block in blocks],
        [ups.at[step] for step in range(2 * pieces)],
        done,
    )
    projected = parts[0][...]
    for part in parts[1:]:
        projected = projected + part[...]
    streams = hidden[...].astype(F32)
    gained = projected * post_gain[...].reshape(1, -1)
    branch[...] = gained
    scale = pre_gain[...].reshape(1, -1)
    operand = jnp.concatenate([(streams * scale).astype(BF), (gained * scale).astype(BF)])
    tile = columns_tile(
        [
            jnp.sum(projected * projected, axis=-1, keepdims=True),
            jnp.sum(streams * gained, axis=-1, keepdims=True),
            jnp.sum(gained * gained, axis=-1, keepdims=True),
        ],
        count,
    )
    coded = split_tile(tile)
    for slot in range(pieces):
        keep[slot, :count, 2 * width :] = tile
        keep[slot, count:, 2 * width :] = jnp.zeros_like(tile)
        send[slot, :count, 2 * width :] = coded
        send[slot, count:, 2 * width :] = jnp.zeros_like(coded)
    for part in range(4 * pieces):
        step, offset = part % (2 * pieces), part // (2 * pieces) * width
        slot = lax.bitwise_xor(place, step % pieces)
        mine = guide == step // pieces
        if offset:
            copies[step].wait()
            product = nn_dot(operand, ups[step])
        else:
            product = nn_dot(operand, gate_weight[:, step * width : (step + 1) * width])

        @pl.when(mine)
        def _(product=product, slot=slot, offset=offset):
            keep[slot, :, offset : offset + width] = product

        @pl.when(jnp.logical_not(mine))
        def _(product=product, slot=slot, offset=offset):
            send[slot, :, offset : offset + width] = product.astype(BF)


def share_kernel(keep, got, own, *outs):
    width = keep.shape[2] - LANES
    count = keep.shape[1] // 2
    tile = keep[0, :count, width:] + joined_tile(got[0, :count, width:])
    own[:, :width] = keep[0, :, :width] + got[0, :, :width].astype(F32)
    own[:count, width:] = tile
    own[count:, width:] = jnp.zeros((count, LANES), F32)
    coded = split_tile(tile)
    for at, out in enumerate(outs):
        out[:, :width] = (
            keep[at + 1, :, :width] + got[at + 1, :, :width].astype(F32)
        ).astype(BF)
        out[:count, width:] = coded
        out[count:, width:] = jnp.zeros_like(coded)


def active_kernel(squares, own, *refs):
    parts, (out, scales) = refs[:-2], refs[-2:]
    count = squares.shape[0]
    width = out.shape[1]
    tile = own[:count, 2 * width :]
    for part in parts:
        tile = tile + joined_tile(part[:count, 2 * width :])
    branch_scale = lax.rsqrt(tile[:, 0:1] / D + EPS)
    middle_sq = squares[:, 0:1] + branch_scale * (
        2.0 * tile[:, 1:2] + branch_scale * tile[:, 2:3]
    )
    scale = lax.rsqrt(jnp.maximum(middle_sq, 0.0) / D + EPS)
    scales[...] = jnp.broadcast_to(branch_scale, (count, LANES))

    def summed(rows, at):
        total = own[rows, at]
        for part in parts:
            total = total + part[rows, at].astype(F32)
        return total

    low, high = slice(0, count), slice(count, 2 * count)
    gate_at, up_at = slice(0, width), slice(width, 2 * width)
    gate = (summed(low, gate_at) + branch_scale * summed(high, gate_at)) * scale
    up = (summed(low, up_at) + branch_scale * summed(high, up_at)) * scale
    out[...] = (jax.nn.gelu(gate, approximate=True) * up).astype(BF)


def down_kernel(pieces, meta, *refs):
    parts, (weight, out) = refs[: 2 * pieces], refs[2 * pieces :]
    units = parts[0].shape[1]
    guide, place = meta[0], meta[2]
    total = jnp.zeros(out.shape, F32)
    for step, part in enumerate(parts):
        side = guide if step < pieces else 1 - guide
        block = side * pieces + lax.bitwise_xor(place, step % pieces)
        held = weight[:, pl.ds(pl.multiple_of(block * units, LANES), units)]
        total = total + nt_dot(part[...], held)
    out[...] = total


def last_kernel(hidden, branch, scales, post_gain, final_gain, *refs):
    parts, out = refs[:-1], refs[-1]
    ffw = parts[0][...]
    for part in parts[1:]:
        ffw = ffw + part[...]
    count = ffw.shape[0]
    middle = hidden[...].astype(F32) + branch[...] * scales[:, 0:1]
    gained = ffw * post_gain[...].reshape(1, -1)
    scale = final_gain[...].reshape(1, -1)
    out[:count, :] = (middle * scale).astype(BF)
    out[count : 2 * count, :] = (gained * scale).astype(BF)
    tile = columns_tile(
        [
            jnp.sum(ffw * ffw, axis=-1, keepdims=True),
            jnp.sum(middle * gained, axis=-1, keepdims=True),
            jnp.sum(gained * gained, axis=-1, keepdims=True),
            jnp.sum(middle * middle, axis=-1, keepdims=True),
        ],
        count,
    )
    out[2 * count :, :LANES] = split_tile(tile)
    out[2 * count :, LANES:] = jnp.zeros((count, out.shape[1] - LANES), BF)


def table_kernel(pieces, meta, *refs):
    parts, (lower, upper, table, keep, send, last, rows, done) = refs[:pieces], refs[pieces:]
    quarter = last.shape[0]
    copies = started([table.at[pl.ds(3 * quarter, quarter)]], [last], done)
    count = parts[0].shape[0] // 3
    half = count // 2
    width = parts[0].shape[1]
    first = meta[0] == 0
    place = meta[2]
    total_rows = 4 * quarter
    for target in range(pieces):
        block = parts[0][: 2 * count, :].astype(F32)
        for at in range(1, pieces):
            block = jnp.where(
                lax.bitwise_xor(place, at) == target,
                parts[at][: 2 * count, :].astype(F32),
                block,
            )
        rows[:, target * width : (target + 1) * width] = block
    tile = joined_tile(parts[0][2 * count :, :LANES])
    for at in range(1, pieces):
        tile = tile + joined_tile(parts[at][2 * count :, :LANES])
    low, high = tile[:half], tile[half:]
    keep[:half, total_rows:] = jnp.where(first, low, high)
    send[:half, total_rows:] = jnp.where(first, high, low)
    keep[half:, total_rows:] = jnp.zeros((half, LANES), F32)
    send[half:, total_rows:] = jnp.zeros((half, LANES), F32)
    operand = rows[...].astype(BF)
    step_rows = quarter // 2
    for block in range(8):
        ref, first_row = ((lower, 0), (upper, 4), (last, 6))[(block >= 4) + (block >= 6)]
        if block == 6:
            copies[0].wait()
        start = (block - first_row) * step_rows
        product = nt_dot(ref[start : start + step_rows, :], operand).T
        at = slice(block * step_rows, (block + 1) * step_rows)
        for base in (0, half):
            low = product[2 * base : 2 * base + half]
            high = product[2 * base + half : 2 * base + 2 * half]
            keep[base : base + half, at] = jnp.where(first, low, high)
            send[base : base + half, at] = jnp.where(first, high, low)


def logits_kernel(places, weights, keep, got, out, mixed):
    rows = keep.shape[0] // 2
    group = rows // 2
    total_rows = keep.shape[1] - LANES
    tile = keep[:rows, total_rows:] + got[:rows, total_rows:]
    branch_scale = lax.rsqrt(tile[:, 0:1] / D + EPS)
    last_sq = tile[:, 3:4] + branch_scale * (
        2.0 * tile[:, 1:2] + branch_scale * tile[:, 2:3]
    )
    scale = lax.rsqrt(jnp.maximum(last_sq, 0.0) / D + EPS)
    sums = keep[:, :total_rows] + got[:, :total_rows]
    logits = LOGIT_CAP * jnp.tanh(
        (sums[:rows] + branch_scale * sums[rows:]) * scale / LOGIT_CAP
    )
    turned = pltpu.roll(logits, group, 0)
    top = lax.broadcasted_iota(jnp.int32, logits.shape, 0) < group
    uncond = jnp.where(top, turned, logits)
    cond = jnp.where(top, logits, turned)
    mixed[...] = uncond + weights[:, 0:1] * (cond - uncond)
    half = places.shape[1]
    for start in range(0, half, LANES):
        at = slice(start, start + LANES)
        wanted = places[:, at]
        lane = lax.bitwise_and(wanted, LANES - 1)
        chunk = lax.shift_right_logical(wanted, 7)
        found = jnp.zeros((rows, LANES), F32)
        for block in range(total_rows // LANES):
            values = mixed[:, block * LANES : (block + 1) * LANES]
            found = jnp.where(
                chunk == block, jnp.take_along_axis(values, lane, axis=1), found
            )
        out[:, start : start + LANES] = found[:group]
        out[:, half + start : half + start + LANES] = found[group:]


def from_peers(value, axis, size):
    values = value if isinstance(value, (list, tuple)) else [value] * (size - 1)
    return [
        lax.ppermute(values[k - 1], axis, [(i, i ^ k) for i in range(size)])
        for k in range(1, size)
    ]


def pair_summed(keep, send):
    return pl.pallas_call(
        pair_kernel,
        out_shape=(
            jax.ShapeDtypeStruct(keep.shape, F32),
            jax.ShapeDtypeStruct(keep.shape, BF),
        ),
        in_specs=[VMEM] * 2,
        out_specs=(VMEM,) * 2,
        compiler_params=limit(16),
    )(keep, from_peers(send, "guide", 2)[0])


def fast_layer(
    hidden,
    lengths,
    slot_owner,
    allowed_ids,
    guidance,
    pre_attn_gain,
    post_attn_gain,
    pre_ffw_gain,
    post_ffw_gain,
    final_gain,
    query_weight,
    key_weight,
    value_weight,
    output_weight,
    gate_weight,
    up_weight,
    down_weight,
    embedding,
    cond_keys,
    cond_values,
    uncond_keys,
    uncond_values,
):
    kinds, requests, width = hidden.shape
    count = kinds * requests
    half = count // 2
    group = half // 2
    heads = query_weight.shape[1] // HD
    kv_heads = key_weight.shape[1] // HD
    seq_size = lax.axis_size("seq")
    kv_size = lax.axis_size("kv")
    guide_index = lax.axis_index("guide")
    seq_index = lax.axis_index("seq")
    kv_index = lax.axis_index("kv")
    place = jnp.stack([guide_index, guide_index * seq_size + seq_index, seq_index]).astype(jnp.int32)
    meta = jnp.concatenate(
        [
            place,
            lengths.reshape(-1),
            slot_owner.reshape(-1),
        ]
    )
    shape = jax.ShapeDtypeStruct

    position = (
        lengths.astype(F32).reshape(kinds, 2, group).transpose(1, 0, 2).reshape(count)
    )
    half_dim = HD // 2
    frequency = THETA ** (-2.0 * jnp.arange(half_dim, dtype=F32) / HD)
    angles = position[:, None] * frequency
    cosine = jnp.cos(angles)
    sine = jnp.sin(angles)
    cosine = jnp.concatenate([cosine, cosine], axis=-1)
    sine = jnp.concatenate([-sine, sine], axis=-1)

    with jax.named_scope("project"):
        joint = (heads + 2 * kv_heads) * HD // 2 + LANES
        rows, keep, send = pl.pallas_call(
            project_kernel,
            out_shape=(
                shape((count, width), BF),
                shape((count, joint), F32),
                shape((count, joint), F32),
            ),
            in_specs=[SMEM] + [ANY] * 5,
            out_specs=(VMEM,) * 3,
            scratch_shapes=[
                pltpu.VMEM(source.shape, source.dtype)
                for source in (hidden.reshape(count, width), pre_attn_gain, query_weight, key_weight, value_weight)
            ]
            + [pltpu.SemaphoreType.DMA((5,))],
            compiler_params=limit(8),
        )(place, *map(in_hbm, (hidden.reshape(count, width), pre_attn_gain, query_weight, key_weight, value_weight)))
        own, coded = pair_summed(keep, send)
        parts = [own] + from_peers(coded, "seq", seq_size)
        mine, squares = pl.pallas_call(
            lambda *refs: rope_kernel(HD, (D // H) ** (-0.5), *refs),
            out_shape=(shape((count, joint - LANES), BF), shape((count, LANES), F32)),
            in_specs=[VMEM] * (2 + seq_size),
            out_specs=(VMEM,) * 2,
            compiler_params=limit(16),
        )(cosine, sine, *parts)
        other = from_peers(mine, "guide", 2)[0]

    with jax.named_scope("attend"):
        attend_width = heads // 2 * HD + LANES
        caches = [cond_keys, cond_values, uncond_keys, uncond_values]
        keep, send = pl.pallas_call(
            attend_kernel,
            out_shape=(shape((count, attend_width), F32),) * 2,
            in_specs=[SMEM] + [VMEM] * 2 + [ANY] * 4,
            out_specs=(VMEM,) * 2,
            scratch_shapes=[pltpu.VMEM(cache.shape, cache.dtype) for cache in caches]
            + [
                pltpu.VMEM((count, heads, kv_heads * HD), F32),
                pltpu.VMEM((count, heads, HD), F32),
                pltpu.VMEM((count, heads, HD), F32),
            ]
            + [pltpu.SemaphoreType.DMA((4 * requests,))],
            compiler_params=limit(28),
        )(meta, mine, other, *map(in_hbm, caches))
        own, coded = pair_summed(keep, send)
        parts = [own] + from_peers(coded, "seq", seq_size)
        mine = pl.pallas_call(
            attended_kernel,
            out_shape=shape((count, heads // 2 * HD), BF),
            in_specs=[VMEM] * seq_size,
            out_specs=VMEM,
            compiler_params=limit(16),
        )(*parts)
        other = from_peers(mine, "guide", 2)[0]
        part = pl.pallas_call(
            output_kernel,
            out_shape=shape((count, width), F32),
            in_specs=[SMEM] + [VMEM] * 3,
            out_specs=VMEM,
            compiler_params=limit(16),
        )(place, mine, other, output_weight.T)
        parts = [part] + from_peers(part, "kv", kv_size)
        near_gate, _ = held_near(part, (gate_weight, 0, width))

    with jax.named_scope("gate_up"):
        hidden_units = gate_weight.shape[1]
        unit_block = hidden_units // (2 * seq_size)
        share_width = 2 * unit_block + LANES
        steps = 2 * seq_size
        keep, send, branch = pl.pallas_call(
            lambda *refs: gate_up_kernel(seq_size, *refs),
            out_shape=(
                shape((seq_size, 2 * count, share_width), F32),
                shape((seq_size, 2 * count, share_width), BF),
                shape((count, width), F32),
            ),
            in_specs=[SMEM] + [VMEM] * (4 + kv_size) + [ANY],
            out_specs=(VMEM,) * 3,
            scratch_shapes=[pltpu.VMEM((steps, width, unit_block), BF)]
            + [pltpu.SemaphoreType.DMA((steps,))],
            compiler_params=limit(16),
        )(place, rows, post_attn_gain, pre_ffw_gain, *parts, near_gate, in_hbm(up_weight))
        got = from_peers(send, "guide", 2)[0]
        own, *shares = pl.pallas_call(
            share_kernel,
            out_shape=(shape((2 * count, share_width), F32),)
            + (shape((2 * count, share_width), BF),) * (seq_size - 1),
            in_specs=[VMEM] * 2,
            out_specs=(VMEM,) * seq_size,
            compiler_params=limit(16),
        )(keep, got)
        parts = from_peers(shares, "seq", seq_size)
        quarter = embedding.shape[0] // 4
        near_down, near_low, token = held_near(
            shares[0], (down_weight.T, 0, width), (embedding, 0, 2 * quarter)
        )
        active, scales = pl.pallas_call(
            lambda token_ref, *refs: active_kernel(*refs),
            out_shape=(shape((count, unit_block), BF), shape((count, LANES), F32)),
            in_specs=[VMEM] * (2 + seq_size),
            out_specs=(VMEM,) * 2,
            compiler_params=limit(16),
        )(token, squares, own, *parts)

    with jax.named_scope("down"):
        mine = [active] + from_peers(active, "seq", seq_size)
        other = [from_peers(value, "guide", 2)[0] for value in mine]
        near_high, _ = held_near(active, (embedding, 2 * quarter, quarter))

        part = pl.pallas_call(
            lambda *refs: down_kernel(seq_size, *refs),
            out_shape=shape((count, width), F32),
            in_specs=[SMEM] + [VMEM] * (1 + steps),
            out_specs=VMEM,
            compiler_params=limit(8),
        )(place, *mine, *other, near_down)
        parts = [part] + from_peers(part, "kv", kv_size)

    with jax.named_scope("head"):
        mine = pl.pallas_call(
            last_kernel,
            out_shape=shape((3 * count, width), BF),
            in_specs=[VMEM] * (5 + kv_size),
            out_specs=VMEM,
            compiler_params=limit(16),
        )(rows, branch, scales, post_ffw_gain, final_gain, *parts)
        parts = [mine] + from_peers(mine, "seq", seq_size)
        table_rows, table_width = embedding.shape
        keep, send = pl.pallas_call(
            lambda *refs: table_kernel(seq_size, *refs),
            out_shape=(shape((count, table_rows + LANES), F32),) * 2,
            in_specs=[SMEM] + [VMEM] * (seq_size + 2) + [ANY],
            out_specs=(VMEM,) * 2,
            scratch_shapes=[
                pltpu.VMEM((quarter, table_width), BF),
                pltpu.VMEM((2 * count, table_width), F32),
                pltpu.SemaphoreType.DMA((1,)),
            ],
            compiler_params=limit(14),
        )(place, *parts, near_low, near_high, in_hbm(embedding))
        got = from_peers(send, "guide", 2)[0]
        allowed = allowed_ids.shape[0]
        places = allowed_ids - (kv_index * seq_size + seq_index) * table_rows
        places = jnp.repeat(places.reshape(2, allowed // 2), group, axis=0)
        weights = lax.dynamic_slice_in_dim(guidance, guide_index * group, group, 0)
        weights = jnp.broadcast_to(jnp.concatenate([weights, weights])[:, None], (half, LANES))
        return pl.pallas_call(
            logits_kernel,
            out_shape=shape((group, allowed), F32),
            in_specs=[VMEM] * 4,
            out_specs=VMEM,
            scratch_shapes=[pltpu.VMEM((half, table_rows), F32)],
            compiler_params=limit(24),
        )(places, weights, keep, got)


def on_device(*arrays):
    units = arrays[14].shape[1] // (2 * lax.axis_size("seq"))
    requests = arrays[0].shape[1]
    if units % LANES or requests != 8 or lax.axis_size("guide") != 2:
        return plain_layer(*arrays)
    return fast_layer(*arrays)


def solution(mesh):
    return jax.shard_map(
        on_device,
        mesh=mesh,
        in_specs=(
            P(None, None, ("guide", "seq")),
            P(),
            P(),
            P(("kv", "seq")),
            P(),
            P(("guide", "seq")),
            P(("guide", "seq")),
            P(("guide", "seq")),
            P(("guide", "seq")),
            P(("guide", "seq")),
            P(("guide", "seq"), "kv"),
            P(("guide", "seq"), "kv"),
            P(("guide", "seq"), "kv"),
            P("kv", ("guide", "seq")),
            P(("guide", "seq"), "kv"),
            P(("guide", "seq"), "kv"),
            P("kv", ("guide", "seq")),
            P(("kv", "seq"), "guide"),
            P(None, ("guide", "seq"), "kv"),
            P(None, ("guide", "seq"), "kv"),
            P(None, ("guide", "seq"), "kv"),
            P(None, ("guide", "seq"), "kv"),
        ),
        out_specs=P("guide", ("kv", "seq")),
        check_vma=False,
    )
```

```python
import jax
import jax.numpy as jnp
from jax import lax
from jax.experimental import pallas as pl
from jax.experimental.pallas import tpu as pltpu
from jax.sharding import PartitionSpec as P

D = 4608
H = 32
HD = 128


EPS = 1e-06
ATTN_CAP = 50.0
LOGIT_CAP = 30.0
THETA = 10000.0
HIGHEST = lax.Precision.HIGHEST


def rotary(values, position):
    half_size = values.shape[-1] // 2
    frequency = THETA ** (-2.0 * jnp.arange(half_size, dtype=jnp.float32) / values.shape[-1])
    angles = position[:, None, None] * frequency
    first_half = values[..., :half_size]
    second_half = values[..., half_size:]
    cosine = jnp.cos(angles)
    sine_part = jnp.sin(angles)
    return jnp.concatenate(
        [
            first_half * cosine - second_half * sine_part,
            second_half * cosine + first_half * sine_part,
        ],
        axis=-1,
    )


def to_slots(slot_pick, array):
    flat = array.astype(jnp.float32).reshape(array.shape[0], array.shape[1], -1)
    moved = jnp.einsum("gsr,gre->gse", slot_pick, flat, precision=HIGHEST)
    return moved.reshape(array.shape).astype(array.dtype)


def to_requests(slot_pick, array):
    flat = array.astype(jnp.float32).reshape(array.shape[0], array.shape[1], -1)
    moved = jnp.einsum("gsr,gse->gre", slot_pick, flat, precision=HIGHEST)
    return moved.reshape(array.shape).astype(array.dtype)


def attend_block(queries, key_block, value_block, slot_len, first_pos, tile_len):
    slot_count, block_len = (key_block.shape[0], key_block.shape[1])
    local_kv, group_size, head_size = (queries.shape[1], queries.shape[2], queries.shape[3])
    live_len = jnp.clip(jnp.max(slot_len) - first_pos, 0, block_len)
    tile_count = (live_len + tile_len - 1) // tile_len

    def one_tile(tile_index, carry):
        numer, denom = carry
        tile_start = tile_index * tile_len
        key_tile = lax.dynamic_slice_in_dim(key_block, tile_start, tile_len, 1).reshape(
            slot_count, tile_len, local_kv, head_size
        )
        value_tile = lax.dynamic_slice_in_dim(value_block, tile_start, tile_len, 1).reshape(
            slot_count, tile_len, local_kv, head_size
        )
        scores = jnp.einsum(
            "rkgd,rtkd->rkgt", queries, key_tile, preferred_element_type=jnp.float32
        )
        places = first_pos + tile_start + jnp.arange(tile_len, dtype=jnp.int32)
        visible = places[None, None, None, :] < slot_len[:, None, None, None]
        probs = jnp.where(visible, jnp.exp(ATTN_CAP * jnp.tanh(scores / ATTN_CAP)), 0.0)
        numer = numer + jnp.einsum(
            "rkgt,rtkd->rkgd",
            probs.astype(jnp.bfloat16),
            value_tile,
            preferred_element_type=jnp.float32,
        )
        denom = denom + jnp.sum(probs, axis=-1)
        return (numer, denom)

    start_numer = jnp.zeros((slot_count, local_kv, group_size, head_size), jnp.float32)
    start_denom = jnp.zeros((slot_count, local_kv, group_size), jnp.float32)
    return lax.fori_loop(0, tile_count, one_tile, (start_numer, start_denom))


def plain_layer(
    hidden,
    lengths,
    slot_owner,
    allowed_ids,
    guidance,
    pre_attn_gain,
    post_attn_gain,
    pre_ffw_gain,
    post_ffw_gain,
    final_gain,
    query_weight,
    key_weight,
    value_weight,
    output_weight,
    gate_weight,
    up_weight,
    down_weight,
    embedding,
    cond_keys,
    cond_values,
    uncond_keys,
    uncond_values,
):
    kinds, requests, width_local = hidden.shape
    stream_count = kinds * requests
    local_heads = query_weight.shape[1] // HD
    local_kv = key_weight.shape[1] // HD
    group_size = local_heads // local_kv
    streams = hidden.astype(jnp.float32)
    normed = (streams * pre_attn_gain).astype(jnp.bfloat16).reshape(stream_count, width_local)
    query_part = jnp.dot(normed, query_weight, preferred_element_type=jnp.float32)
    key_part = jnp.dot(normed, key_weight, preferred_element_type=jnp.float32)
    value_part = jnp.dot(normed, value_weight, preferred_element_type=jnp.float32)
    square_part = jnp.sum(streams * streams, axis=-1)
    square_sum, query_sum, key_sum, value_sum = lax.psum(
        (square_part, query_part, key_part, value_part), ("guide", "seq")
    )
    row_scale = lax.rsqrt(square_sum / D + EPS).reshape(stream_count, 1)
    position = lengths.astype(jnp.float32).reshape(stream_count)
    queries = (
        rotary((query_sum * row_scale).reshape(stream_count, local_heads, HD), position)
        * (D // H) ** (-0.5)
    ).astype(jnp.bfloat16)
    new_keys = rotary((key_sum * row_scale).reshape(stream_count, local_kv, HD), position).astype(
        jnp.bfloat16
    )
    new_values = (value_sum * row_scale).astype(jnp.bfloat16)
    queries = queries.reshape(kinds, requests, local_kv, group_size, HD)
    new_keys = new_keys.reshape(kinds, requests, local_kv, HD)
    new_values = new_values.reshape(kinds, requests, local_kv, HD)
    matches = slot_owner[:, :, None] == jnp.arange(requests, dtype=jnp.int32)[None, None, :]
    slot_pick = matches.astype(jnp.float32)
    slot_len = jnp.sum(jnp.where(matches, lengths[:, None, :], 0), axis=-1)
    slot_queries = to_slots(slot_pick, queries)
    slot_keys = to_slots(slot_pick, new_keys)
    slot_values = to_slots(slot_pick, new_values)
    guide_index = lax.axis_index("guide")
    seq_index = lax.axis_index("seq")
    block_index = guide_index * lax.axis_size("seq") + seq_index
    cond_len = cond_keys.shape[1]
    uncond_len = uncond_keys.shape[1]
    cond_numer, cond_denom = attend_block(
        slot_queries[0],
        cond_keys,
        cond_values,
        slot_len[0],
        block_index * cond_len,
        min(256, cond_len),
    )
    uncond_numer, uncond_denom = attend_block(
        slot_queries[1],
        uncond_keys,
        uncond_values,
        slot_len[1],
        block_index * uncond_len,
        min(256, uncond_len),
    )
    numer_part = jnp.stack([cond_numer, uncond_numer])
    denom_part = jnp.stack([cond_denom, uncond_denom])
    numer_sum, denom_sum = lax.psum((numer_part, denom_part), ("guide", "seq"))
    own_score = jnp.einsum(
        "gskjd,gskd->gskj", slot_queries, slot_keys, preferred_element_type=jnp.float32
    )
    own_prob = jnp.exp(ATTN_CAP * jnp.tanh(own_score / ATTN_CAP))
    own_weight = own_prob.astype(jnp.bfloat16).astype(jnp.float32)
    numer_total = (
        numer_sum + own_weight[..., None] * slot_values.astype(jnp.float32)[:, :, :, None, :]
    )
    denom_total = denom_sum + own_prob
    attended_slots = (numer_total / denom_total[..., None]).astype(jnp.bfloat16)
    attended = to_requests(slot_pick, attended_slots).reshape(stream_count, local_heads * HD)
    out_part = jnp.dot(attended, output_weight, preferred_element_type=jnp.float32)
    projected = lax.psum(out_part, "kv").reshape(kinds, requests, width_local)
    branch_sq = lax.psum(jnp.sum(projected * projected, axis=-1), ("guide", "seq"))
    out_scale = lax.rsqrt(branch_sq / D + EPS)
    middle = streams + projected * out_scale[..., None] * post_attn_gain
    middle_sq = lax.psum(jnp.sum(middle * middle, axis=-1), ("guide", "seq"))
    ffw_in = (middle * pre_ffw_gain).astype(jnp.bfloat16).reshape(stream_count, width_local)
    ffw_scale = lax.rsqrt(middle_sq / D + EPS).reshape(stream_count, 1)
    gate_part = jnp.dot(ffw_in, gate_weight, preferred_element_type=jnp.float32)
    upward_part = jnp.dot(ffw_in, up_weight, preferred_element_type=jnp.float32)
    gate_sum, upward_sum = lax.psum((gate_part, upward_part), ("guide", "seq"))
    activ = (jax.nn.gelu(gate_sum * ffw_scale, approximate=True) * (upward_sum * ffw_scale)).astype(
        jnp.bfloat16
    )
    down_part = jnp.dot(activ, down_weight, preferred_element_type=jnp.float32)
    ffw_out = lax.psum(down_part, "kv").reshape(kinds, requests, width_local)
    ffw_sq = lax.psum(jnp.sum(ffw_out * ffw_out, axis=-1), ("guide", "seq"))
    branch_scale = lax.rsqrt(ffw_sq / D + EPS)
    last = middle + ffw_out * branch_scale[..., None] * post_ffw_gain
    last_sq = lax.psum(jnp.sum(last * last, axis=-1), ("guide", "seq"))
    final_scale = lax.rsqrt(last_sq / D + EPS)
    final_rows = (last * final_gain).astype(jnp.bfloat16)
    half_rows = lax.all_gather(final_rows, "seq", axis=2, tiled=True)
    table_rows = embedding.shape[0]
    block_first = (lax.axis_index("kv") * lax.axis_size("seq") + seq_index) * table_rows
    picked = jnp.take(embedding, allowed_ids - block_first, axis=0)
    logit_part = jnp.einsum(
        "sd,ad->sa",
        half_rows.reshape(stream_count, half_rows.shape[2]),
        picked,
        preferred_element_type=jnp.float32,
    )
    logit_term = jnp.transpose(logit_part.reshape(kinds, requests, picked.shape[0]), (1, 0, 2))
    logit_share = lax.psum_scatter(logit_term, "guide", scatter_dimension=0, tiled=True)
    half_req = requests // 2
    first_req = guide_index * half_req
    share_scale = jnp.transpose(
        lax.dynamic_slice_in_dim(final_scale, first_req, half_req, 1), (1, 0)
    )
    capped = LOGIT_CAP * jnp.tanh(logit_share * share_scale[:, :, None] / LOGIT_CAP)
    share_weight = lax.dynamic_slice_in_dim(guidance, first_req, half_req, 0)
    return capped[:, 1] + share_weight[:, None] * (capped[:, 0] - capped[:, 1])


BF = jnp.bfloat16
F32 = jnp.float32
LANES = 128
ANY = pl.BlockSpec(memory_space=pl.ANY)
VMEM = pl.BlockSpec(memory_space=pltpu.VMEM)
SMEM = pl.BlockSpec(memory_space=pltpu.SMEM)
MIB = 1 << 20
COPIES = 4
AHEAD = 5


def nt_dot(a, b):
    return lax.dot_general(a, b, (((1,), (1,)), ((), ())), preferred_element_type=F32)


def nn_dot(a, b):
    return jnp.dot(a, b, preferred_element_type=F32)


def in_hbm(value):
    return pltpu.with_memory_space_constraint(value, pltpu.HBM)


def started(sources, targets, done):
    copies = [
        pltpu.make_async_copy(source, target, done.at[at])
        for at, (source, target) in enumerate(zip(sources, targets))
    ]
    for copy in copies:
        copy.start()
    return copies


def limit(mib):
    return pltpu.CompilerParams(vmem_limit_bytes=mib * MIB)


def columns_tile(values, rows):
    lane = lax.broadcasted_iota(jnp.int32, (rows, LANES), 1)
    tile = jnp.zeros((rows, LANES), F32)
    for place, value in enumerate(values):
        tile = jnp.where(lane == place, value, tile)
    return tile


def split_tile(tile):
    high = tile.astype(BF).astype(F32)
    rest = tile - high
    middle = rest.astype(BF).astype(F32)
    low = (rest - middle).astype(BF).astype(F32)
    return (high + pltpu.roll(middle, 32, 1) + pltpu.roll(low, 64, 1)).astype(BF)


def joined_tile(tile):
    terms = tile.astype(F32)
    total = terms + pltpu.roll(terms, LANES - 32, 1) + pltpu.roll(terms, LANES - 64, 1)
    lane = lax.broadcasted_iota(jnp.int32, total.shape, 1)
    return jnp.where(lane < 32, total, 0.0)


def project_kernel(meta, *refs):
    sources, (rows, keep, send), held, done = refs[:5], refs[5:8], refs[8:13], refs[13]
    copies = started(sources, held, done)
    hidden, gain, *weights = held
    for copy in copies[:2]:
        copy.wait()
    count = hidden.shape[0]
    half = count // 2
    group = half // 2
    row = lax.broadcasted_iota(jnp.int32, (count, count), 0)
    column = lax.broadcasted_iota(jnp.int32, (count, count), 1)
    source = (row // group) % 2 * half + row // half * group + row % group
    pick = jnp.where(column == source, 1.0, 0.0).astype(BF)
    streams = nn_dot(pick, hidden[...])
    rows[...] = streams.astype(BF)
    square = jnp.sum(streams * streams, axis=-1, keepdims=True)
    normed = (streams * gain[...].reshape(1, -1)).astype(BF)
    first = meta[0] == 0
    offset = 0
    for copy, weight in zip(copies[2:], weights):
        copy.wait()
        product = nn_dot(normed, weight[...])
        width = product.shape[1] // 2
        low, high = product[:, :width], product[:, width:]
        keep[:, offset : offset + width] = jnp.where(first, low, high)
        send[:, offset : offset + width] = jnp.where(first, high, low)
        offset += width
    tile = columns_tile([square], count)
    keep[:, offset:] = tile
    send[:, offset:] = tile


def hold_kernel(starts, *refs):
    count = len(starts)
    sources, (*targets, token, done) = refs[1 : count + 1], refs[count + 1 :]
    token[...] = jnp.zeros_like(token)
    pieces = []
    for start, source, target in zip(starts, sources, targets):
        if source.shape[1:] != target.shape[1:]:
            source = source.at[:, pl.ds(0, target.shape[1])]
        size = target.shape[0] // COPIES
        pieces += [
            (source.at[pl.ds(start + at * size, size)], target.at[pl.ds(at * size, size)])
            for at in range(COPIES)
        ]
    for copy in started(*zip(*pieces), done):
        copy.wait()


def held_near(after, *values, columns=None):
    arrays = [array for array, _, _ in values]
    starts = [start for _, start, _ in values]
    shapes = [
        (rows,) + ((columns,) if columns else array.shape[1:]) for array, _, rows in values
    ]
    size = sum(2 * rows * held[-1] for (_, _, rows), held in zip(values, shapes))
    return pl.pallas_call(
        lambda *refs: hold_kernel(starts, *refs),
        out_shape=[pltpu.VMEM(held, array.dtype) for held, array in zip(shapes, arrays)]
        + [jax.ShapeDtypeStruct((8, LANES), F32)],
        in_specs=[ANY] * (1 + len(values)),
        out_specs=[VMEM] * (1 + len(values)),
        scratch_shapes=[pltpu.SemaphoreType.DMA((COPIES * len(values),))],
        cost_estimate=pl.CostEstimate(flops=0, bytes_accessed=2 * size, transcendentals=0),
        compiler_params=limit(2),
    )(after, *map(in_hbm, arrays))


def pair_kernel(keep, got, own, coded):
    total = keep[...] + got[...]
    own[...] = total
    width = total.shape[1] - LANES
    coded[:, :width] = total[:, :width].astype(BF)
    coded[:, width:] = split_tile(total[:, width:])


def added_parts(own, parts):
    width = own.shape[1] - LANES
    total, tile = own[:, :width], own[:, width:]
    for part in parts:
        total = total + part[:, :width].astype(F32)
        tile = tile + joined_tile(part[:, width:])
    return total, tile


def rope_kernel(head_dim, scale, cosine, sine, *refs):
    parts, (out, squares) = refs[:-2], refs[-2:]
    total, tile = added_parts(parts[0], parts[1:])
    blocks = total.shape[1] // head_dim
    squares[...] = tile
    row_scale = lax.rsqrt(tile[:, :1] / D + EPS)
    cosines, sines = cosine[...], sine[...]
    for block in range(blocks):
        entry = total[:, block * head_dim : (block + 1) * head_dim] * row_scale
        if block < blocks * 3 // 4:
            entry = entry * cosines + pltpu.roll(entry, head_dim // 2, 1) * sines
        if block < blocks // 2:
            entry = entry * scale
        out[:, block * head_dim : (block + 1) * head_dim] = entry.astype(BF)


def attend_kernel(meta, mine, other, *refs):
    sources, (keep, send), held = refs[:4], refs[4:6], refs[6:10]
    queries, numer, denom, done = refs[10:]
    slots = sources[0].shape[0]
    order = [(slot, which) for slot in range(slots) for which in (0, 2, 1, 3)]
    copies = started(
        [sources[which].at[slot] for slot, which in order],
        [held[which].at[slot] for slot, which in order],
        done,
    )
    arrived = dict(zip(order, copies))
    count, heads, wide = queries.shape
    head_dim = numer.shape[2]
    half = count // 2
    group = half // 2
    half_heads = heads // 2
    half_kv = half_heads // 2
    first = meta[0] == 0
    block_index = meta[1]

    def piece(index, at):
        a = mine[:, at * head_dim : (at + 1) * head_dim].astype(F32)
        b = other[:, at * head_dim : (at + 1) * head_dim].astype(F32)
        return jnp.where(first, a, b) if index == 0 else jnp.where(first, b, a)

    queries[...] = jnp.zeros_like(queries)
    for head in range(heads):
        kv = head // 2
        queries[:, head, kv * head_dim : (kv + 1) * head_dim] = piece(
            head // half_heads, head % half_heads
        )

    def place_of(kind, slot):
        request = meta[3 + (2 + kind) * half + slot]
        row = request // group * half + kind * group + request % group
        return row, meta[3 + kind * half + request]

    def scores_of(kind, slot):
        row, length = place_of(kind, slot)
        query = queries[row].astype(BF)
        scores = nt_dot(query, held[2 * kind][slot])
        place = block_index * scores.shape[1] + lax.broadcasted_iota(jnp.int32, scores.shape, 1)
        return jnp.where(
            place < length, jnp.exp(ATTN_CAP * jnp.tanh(scores / ATTN_CAP)), 0.0
        )

    head_row = lax.broadcasted_iota(jnp.int32, (heads, head_dim), 0)

    def weigh(kind, slot, probs):
        row, _ = place_of(kind, slot)
        sums = nn_dot(probs.astype(BF), held[2 * kind + 1][slot])
        folded = jnp.zeros((heads, head_dim), F32)
        for kv in range(heads // 2):
            folded = jnp.where(
                head_row // 2 == kv, sums[:, kv * head_dim : (kv + 1) * head_dim], folded
            )
        numer[row] = folded
        denom[row] = jnp.broadcast_to(
            jnp.sum(probs, axis=-1, keepdims=True), (heads, head_dim)
        )

    ready = None
    for slot in range(slots + 1):
        if slot < slots:
            arrived[slot, 0].wait()
            arrived[slot, 2].wait()
        if slot > 0:
            arrived[slot - 1, 1].wait()
            arrived[slot - 1, 3].wait()
        following = [scores_of(kind, slot) for kind in (0, 1)] if slot < slots else None
        if ready is not None:
            for kind in (0, 1):
                weigh(kind, slot - 1, ready[kind])
        ready = following

    owned = jnp.where(block_index == 0, 1.0, 0.0)
    sums, totals = [], []
    for head in range(heads):
        side = head // half_heads
        kv = head % half_heads // 2
        query = piece(side, head % half_heads)
        key = piece(side, half_heads + kv)
        value = piece(side, half_heads + half_kv + kv)
        score = jnp.sum(query * key, axis=-1, keepdims=True)
        own = jnp.exp(ATTN_CAP * jnp.tanh(score / ATTN_CAP))
        weight = own.astype(BF).astype(F32)
        sums.append(numer[:, head, :] + owned * weight * value)
        totals.append(denom[:, head, :1] + owned * own)
    for at in range(half_heads):
        low, high = sums[at], sums[half_heads + at]
        keep[:, at * head_dim : (at + 1) * head_dim] = jnp.where(first, low, high)
        send[:, at * head_dim : (at + 1) * head_dim] = jnp.where(first, high, low)
    low = columns_tile(totals[:half_heads], count)
    high = columns_tile(totals[half_heads:], count)
    keep[:, half_heads * head_dim :] = jnp.where(first, low, high)
    send[:, half_heads * head_dim :] = jnp.where(first, high, low)


def attended_kernel(*refs):
    parts, out = refs[:-1], refs[-1]
    total, tile = added_parts(parts[0], parts[1:])
    for head in range(out.shape[1] // HD):
        at = slice(head * HD, (head + 1) * HD)
        out[:, at] = (total[:, at] / tile[:, head : head + 1]).astype(BF)


def output_kernel(meta, mine, other, weight, out):
    first = meta[0] == 0
    a, b = mine[...].astype(F32), other[...].astype(F32)
    low = jnp.where(first, a, b).astype(BF)
    high = jnp.where(first, b, a).astype(BF)
    width = mine.shape[1]
    out[...] = nt_dot(low, weight[:, :width]) + nt_dot(high, weight[:, width:])


def gate_up_kernel(pieces, meta, hidden, post_gain, pre_gain, *refs):
    parts, (near_gate, gate_weight, up_weight, keep, send, branch, held, done) = refs[:-8], refs[-8:]
    count = hidden.shape[0]
    width = held.shape[2]
    guide, place = meta[0], meta[2]
    steps = 2 * pieces
    near = near_gate.shape[1] // width
    far = [(gate_weight, step) for step in range(near, steps)]
    far += [(up_weight, step) for step in range(steps)]
    copies = [
        pltpu.make_async_copy(
            weight.at[:, pl.ds(step * width, width)], held.at[at], done.at[at]
        )
        for at, (weight, step) in enumerate(far)
    ]
    for copy in copies[:AHEAD]:
        copy.start()
    projected = parts[0][...]
    for part in parts[1:]:
        projected = projected + part[...]
    streams = hidden[...].astype(F32)
    gained = projected * post_gain[...].reshape(1, -1)
    branch[...] = gained
    scale = pre_gain[...].reshape(1, -1)
    operand = jnp.concatenate([(streams * scale).astype(BF), (gained * scale).astype(BF)])
    tile = columns_tile(
        [
            jnp.sum(projected * projected, axis=-1, keepdims=True),
            jnp.sum(streams * gained, axis=-1, keepdims=True),
            jnp.sum(gained * gained, axis=-1, keepdims=True),
        ],
        count,
    )
    coded = split_tile(tile)
    for slot in range(pieces):
        keep[slot, :count, 2 * width :] = tile
        keep[slot, count:, 2 * width :] = jnp.zeros_like(tile)
        send[slot, :count, 2 * width :] = coded
        send[slot, count:, 2 * width :] = jnp.zeros_like(coded)
    for part in range(2 * steps):
        step, offset = part % steps, part // steps * width
        slot = lax.bitwise_xor(place, step % pieces)
        mine = guide == step // pieces
        if part < near:
            product = nn_dot(operand, near_gate[:, step * width : (step + 1) * width])
        else:
            copies[part - near].wait()
            if part - near + AHEAD < len(copies):
                copies[part - near + AHEAD].start()
            product = nn_dot(operand, held[part - near])

        @pl.when(mine)
        def _(product=product, slot=slot, offset=offset):
            keep[slot, :, offset : offset + width] = product

        @pl.when(jnp.logical_not(mine))
        def _(product=product, slot=slot, offset=offset):
            send[slot, :, offset : offset + width] = product.astype(BF)


def share_kernel(keep, got, own, *outs):
    width = keep.shape[2] - LANES
    count = keep.shape[1] // 2
    tile = keep[0, :count, width:] + joined_tile(got[0, :count, width:])
    own[:, :width] = keep[0, :, :width] + got[0, :, :width].astype(F32)
    own[:count, width:] = tile
    own[count:, width:] = jnp.zeros((count, LANES), F32)
    coded = split_tile(tile)
    for at, out in enumerate(outs):
        out[:, :width] = (
            keep[at + 1, :, :width] + got[at + 1, :, :width].astype(F32)
        ).astype(BF)
        out[:count, width:] = coded
        out[count:, width:] = jnp.zeros_like(coded)


def active_kernel(squares, own, *refs):
    parts, (out, scales) = refs[:-2], refs[-2:]
    count = squares.shape[0]
    width = out.shape[1]
    tile = own[:count, 2 * width :]
    for part in parts:
        tile = tile + joined_tile(part[:count, 2 * width :])
    branch_scale = lax.rsqrt(tile[:, 0:1] / D + EPS)
    middle_sq = squares[:, 0:1] + branch_scale * (
        2.0 * tile[:, 1:2] + branch_scale * tile[:, 2:3]
    )
    scale = lax.rsqrt(jnp.maximum(middle_sq, 0.0) / D + EPS)
    scales[...] = jnp.broadcast_to(branch_scale, (count, LANES))

    def summed(rows, at):
        total = own[rows, at]
        for part in parts:
            total = total + part[rows, at].astype(F32)
        return total

    low, high = slice(0, count), slice(count, 2 * count)
    gate_at, up_at = slice(0, width), slice(width, 2 * width)
    gate = (summed(low, gate_at) + branch_scale * summed(high, gate_at)) * scale
    up = (summed(low, up_at) + branch_scale * summed(high, up_at)) * scale
    out[...] = (jax.nn.gelu(gate, approximate=True) * up).astype(BF)


def by_distance(parts):
    return parts[:1] + parts[:0:-1]


def down_kernel(pieces, meta, *refs):
    parts = by_distance(refs[:pieces]) + by_distance(refs[pieces : 2 * pieces])
    weight, out = refs[2 * pieces :]
    units = parts[0].shape[1]
    guide, place = meta[0], meta[2]
    total = jnp.zeros(out.shape, F32)
    for step, part in enumerate(parts):
        side = guide if step < pieces else 1 - guide
        block = side * pieces + lax.bitwise_xor(place, step % pieces)
        held = weight[:, pl.ds(pl.multiple_of(block * units, LANES), units)]
        total = total + nt_dot(part[...], held)
    out[...] = total


def last_kernel(hidden, branch, scales, post_gain, final_gain, *refs):
    parts, out = refs[:-1], refs[-1]
    ffw = parts[0][...]
    for part in parts[1:]:
        ffw = ffw + part[...]
    count = ffw.shape[0]
    middle = hidden[...].astype(F32) + branch[...] * scales[:, 0:1]
    gained = ffw * post_gain[...].reshape(1, -1)
    scale = final_gain[...].reshape(1, -1)
    out[:count, :] = (middle * scale).astype(BF)
    out[count : 2 * count, :] = (gained * scale).astype(BF)
    tile = columns_tile(
        [
            jnp.sum(ffw * ffw, axis=-1, keepdims=True),
            jnp.sum(middle * gained, axis=-1, keepdims=True),
            jnp.sum(gained * gained, axis=-1, keepdims=True),
            jnp.sum(middle * middle, axis=-1, keepdims=True),
        ],
        count,
    )
    out[2 * count :, :LANES] = split_tile(tile)
    out[2 * count :, LANES:] = jnp.zeros((count, out.shape[1] - LANES), BF)


def table_kernel(pieces, meta, *refs):
    parts, (lower, middle, upper, table, keep, send, last, rows, done) = refs[:pieces], refs[pieces:]
    parts = by_distance(parts)
    quarter = last.shape[0]
    copies = started([table.at[pl.ds(3 * quarter, quarter)]], [last], done)
    count = parts[0].shape[0] // 3
    half = count // 2
    width = parts[0].shape[1]
    first = meta[0] == 0
    place = meta[2]
    total_rows = 4 * quarter
    for target in range(pieces):
        block = parts[0][: 2 * count, :].astype(F32)
        for at in range(1, pieces):
            block = jnp.where(
                lax.bitwise_xor(place, at) == target,
                parts[at][: 2 * count, :].astype(F32),
                block,
            )
        rows[:, target * width : (target + 1) * width] = block
    tile = joined_tile(parts[0][2 * count :, :LANES])
    for at in range(1, pieces):
        tile = tile + joined_tile(parts[at][2 * count :, :LANES])
    low, high = tile[:half], tile[half:]
    keep[:half, total_rows:] = jnp.where(first, low, high)
    send[:half, total_rows:] = jnp.where(first, high, low)
    keep[half:, total_rows:] = jnp.zeros((half, LANES), F32)
    send[half:, total_rows:] = jnp.zeros((half, LANES), F32)
    operand = rows[...].astype(BF)
    step_rows = quarter // 2
    for block in range(8):
        ref, first_row = ((lower, 0), (middle, 4), (upper, 5), (last, 6))[
            (block >= 4) + (block >= 5) + (block >= 6)
        ]
        if block == 6:
            copies[0].wait()
        start = (block - first_row) * step_rows
        product = nt_dot(ref[start : start + step_rows, :], operand).T
        at = slice(block * step_rows, (block + 1) * step_rows)
        for base in (0, half):
            low = product[2 * base : 2 * base + half]
            high = product[2 * base + half : 2 * base + 2 * half]
            keep[base : base + half, at] = jnp.where(first, low, high)
            send[base : base + half, at] = jnp.where(first, high, low)


def logits_kernel(places, weights, keep, got, out, mixed):
    rows = keep.shape[0] // 2
    group = rows // 2
    total_rows = keep.shape[1] - LANES
    tile = keep[:rows, total_rows:] + got[:rows, total_rows:]
    branch_scale = lax.rsqrt(tile[:, 0:1] / D + EPS)
    last_sq = tile[:, 3:4] + branch_scale * (
        2.0 * tile[:, 1:2] + branch_scale * tile[:, 2:3]
    )
    scale = lax.rsqrt(jnp.maximum(last_sq, 0.0) / D + EPS)
    sums = keep[:, :total_rows] + got[:, :total_rows]
    logits = LOGIT_CAP * jnp.tanh(
        (sums[:rows] + branch_scale * sums[rows:]) * scale / LOGIT_CAP
    )
    turned = pltpu.roll(logits, group, 0)
    top = lax.broadcasted_iota(jnp.int32, logits.shape, 0) < group
    uncond = jnp.where(top, turned, logits)
    cond = jnp.where(top, logits, turned)
    mixed[...] = uncond + weights[:, 0:1] * (cond - uncond)
    half = places.shape[1]
    for start in range(0, half, LANES):
        at = slice(start, start + LANES)
        wanted = places[:, at]
        lane = lax.bitwise_and(wanted, LANES - 1)
        chunk = lax.shift_right_logical(wanted, 7)
        found = jnp.zeros((rows, LANES), F32)
        for block in range(total_rows // LANES):
            values = mixed[:, block * LANES : (block + 1) * LANES]
            found = jnp.where(
                chunk == block, jnp.take_along_axis(values, lane, axis=1), found
            )
        out[:, start : start + LANES] = found[:group]
        out[:, half + start : half + start + LANES] = found[group:]


def from_peers(value, axis, size):
    values = value if isinstance(value, (list, tuple)) else [value] * (size - 1)
    return [
        lax.ppermute(values[k - 1], axis, [(i, i ^ k) for i in range(size)])
        for k in range(size - 1, 0, -1)
    ]


def pair_summed(keep, send):
    return pl.pallas_call(
        pair_kernel,
        out_shape=(
            jax.ShapeDtypeStruct(keep.shape, F32),
            jax.ShapeDtypeStruct(keep.shape, BF),
        ),
        in_specs=[VMEM] * 2,
        out_specs=(VMEM,) * 2,
        compiler_params=limit(16),
    )(keep, from_peers(send, "guide", 2)[0])


def fast_layer(
    hidden,
    lengths,
    slot_owner,
    allowed_ids,
    guidance,
    pre_attn_gain,
    post_attn_gain,
    pre_ffw_gain,
    post_ffw_gain,
    final_gain,
    query_weight,
    key_weight,
    value_weight,
    output_weight,
    gate_weight,
    up_weight,
    down_weight,
    embedding,
    cond_keys,
    cond_values,
    uncond_keys,
    uncond_values,
):
    kinds, requests, width = hidden.shape
    count = kinds * requests
    half = count // 2
    group = half // 2
    heads = query_weight.shape[1] // HD
    kv_heads = key_weight.shape[1] // HD
    seq_size = lax.axis_size("seq")
    kv_size = lax.axis_size("kv")
    guide_index = lax.axis_index("guide")
    seq_index = lax.axis_index("seq")
    kv_index = lax.axis_index("kv")
    place = jnp.stack([guide_index, guide_index * seq_size + seq_index, seq_index]).astype(jnp.int32)
    meta = jnp.concatenate(
        [
            place,
            lengths.reshape(-1),
            slot_owner.reshape(-1),
        ]
    )
    shape = jax.ShapeDtypeStruct

    position = (
        lengths.astype(F32).reshape(kinds, 2, group).transpose(1, 0, 2).reshape(count)
    )
    half_dim = HD // 2
    frequency = THETA ** (-2.0 * jnp.arange(half_dim, dtype=F32) / HD)
    angles = position[:, None] * frequency
    cosine = jnp.cos(angles)
    sine = jnp.sin(angles)
    cosine = jnp.concatenate([cosine, cosine], axis=-1)
    sine = jnp.concatenate([-sine, sine], axis=-1)

    with jax.named_scope("project"):
        joint = (heads + 2 * kv_heads) * HD // 2 + LANES
        rows, keep, send = pl.pallas_call(
            project_kernel,
            out_shape=(
                shape((count, width), BF),
                shape((count, joint), F32),
                shape((count, joint), F32),
            ),
            in_specs=[SMEM] + [ANY] * 5,
            out_specs=(VMEM,) * 3,
            scratch_shapes=[
                pltpu.VMEM(source.shape, source.dtype)
                for source in (hidden.reshape(count, width), pre_attn_gain, query_weight, key_weight, value_weight)
            ]
            + [pltpu.SemaphoreType.DMA((5,))],
            compiler_params=limit(8),
        )(place, *map(in_hbm, (hidden.reshape(count, width), pre_attn_gain, query_weight, key_weight, value_weight)))
        own, coded = pair_summed(keep, send)
        parts = [own] + from_peers(coded, "seq", seq_size)
        mine, squares = pl.pallas_call(
            lambda *refs: rope_kernel(HD, (D // H) ** (-0.5), *refs),
            out_shape=(shape((count, joint - LANES), BF), shape((count, LANES), F32)),
            in_specs=[VMEM] * (2 + seq_size),
            out_specs=(VMEM,) * 2,
            compiler_params=limit(16),
        )(cosine, sine, *parts)
        other = from_peers(mine, "guide", 2)[0]

    with jax.named_scope("attend"):
        attend_width = heads // 2 * HD + LANES
        caches = [cond_keys, cond_values, uncond_keys, uncond_values]
        keep, send = pl.pallas_call(
            attend_kernel,
            out_shape=(shape((count, attend_width), F32),) * 2,
            in_specs=[SMEM] + [VMEM] * 2 + [ANY] * 4,
            out_specs=(VMEM,) * 2,
            scratch_shapes=[pltpu.VMEM(cache.shape, cache.dtype) for cache in caches]
            + [
                pltpu.VMEM((count, heads, kv_heads * HD), F32),
                pltpu.VMEM((count, heads, HD), F32),
                pltpu.VMEM((count, heads, HD), F32),
            ]
            + [pltpu.SemaphoreType.DMA((4 * requests,))],
            compiler_params=limit(28),
        )(meta, mine, other, *map(in_hbm, caches))
        own, coded = pair_summed(keep, send)
        parts = [own] + from_peers(coded, "seq", seq_size)
        mine = pl.pallas_call(
            attended_kernel,
            out_shape=shape((count, heads // 2 * HD), BF),
            in_specs=[VMEM] * seq_size,
            out_specs=VMEM,
            compiler_params=limit(16),
        )(*parts)
        other = from_peers(mine, "guide", 2)[0]
        part = pl.pallas_call(
            output_kernel,
            out_shape=shape((count, width), F32),
            in_specs=[SMEM] + [VMEM] * 3,
            out_specs=VMEM,
            compiler_params=limit(16),
        )(place, mine, other, output_weight.T)
        parts = [part] + from_peers(part, "kv", kv_size)
        near_gate, _ = held_near(
            part, (gate_weight, 0, width), columns=3 * gate_weight.shape[1] // 4
        )

    with jax.named_scope("gate_up"):
        hidden_units = gate_weight.shape[1]
        unit_block = hidden_units // (2 * seq_size)
        share_width = 2 * unit_block + LANES
        steps = 2 * seq_size
        keep, send, branch = pl.pallas_call(
            lambda *refs: gate_up_kernel(seq_size, *refs),
            out_shape=(
                shape((seq_size, 2 * count, share_width), F32),
                shape((seq_size, 2 * count, share_width), BF),
                shape((count, width), F32),
            ),
            in_specs=[SMEM] + [VMEM] * (4 + kv_size) + [ANY] * 2,
            out_specs=(VMEM,) * 3,
            scratch_shapes=[
                pltpu.VMEM((steps * 5 // 4, width, unit_block), BF),
                pltpu.SemaphoreType.DMA((steps * 5 // 4,)),
            ],
            compiler_params=limit(18),
        )(place, rows, post_attn_gain, pre_ffw_gain, *parts, near_gate, in_hbm(gate_weight), in_hbm(up_weight))
        got = from_peers(send, "guide", 2)[0]
        own, *shares = pl.pallas_call(
            share_kernel,
            out_shape=(shape((2 * count, share_width), F32),)
            + (shape((2 * count, share_width), BF),) * (seq_size - 1),
            in_specs=[VMEM] * 2,
            out_specs=(VMEM,) * seq_size,
            compiler_params=limit(16),
        )(keep, got)
        parts = from_peers(shares, "seq", seq_size)
        parts = parts[1:2] + parts[:1] + parts[2:]
        quarter = embedding.shape[0] // 4
        near_down, near_low, token = held_near(
            shares[0], (down_weight.T, 0, width), (embedding, 0, 2 * quarter)
        )
        active, scales = pl.pallas_call(
            lambda token_ref, *refs: active_kernel(*refs),
            out_shape=(shape((count, unit_block), BF), shape((count, LANES), F32)),
            in_specs=[VMEM] * (2 + seq_size),
            out_specs=(VMEM,) * 2,
            compiler_params=limit(16),
        )(token, squares, own, *parts)

    with jax.named_scope("down"):
        mine = [active] + from_peers(active, "seq", seq_size)
        other = [from_peers(value, "guide", 2)[0] for value in mine]

        part = pl.pallas_call(
            lambda *refs: down_kernel(seq_size, *refs),
            out_shape=shape((count, width), F32),
            in_specs=[SMEM] + [VMEM] * (1 + steps),
            out_specs=VMEM,
            compiler_params=limit(8),
        )(place, *mine, *other, near_down)
        parts = [part] + from_peers(part, "kv", kv_size)
        near_middle, token = held_near(part, (embedding, 2 * quarter, quarter // 2))

    with jax.named_scope("head"):
        mine = pl.pallas_call(
            lambda token_ref, *refs: last_kernel(*refs),
            out_shape=shape((3 * count, width), BF),
            in_specs=[VMEM] * (6 + kv_size),
            out_specs=VMEM,
            compiler_params=limit(16),
        )(token, rows, branch, scales, post_ffw_gain, final_gain, *parts)
        parts = [mine] + from_peers(mine, "seq", seq_size)
        near_high, _ = held_near(mine, (embedding, 5 * quarter // 2, quarter // 2))
        table_rows, table_width = embedding.shape
        keep, send = pl.pallas_call(
            lambda *refs: table_kernel(seq_size, *refs),
            out_shape=(shape((count, table_rows + LANES), F32),) * 2,
            in_specs=[SMEM] + [VMEM] * (seq_size + 3) + [ANY],
            out_specs=(VMEM,) * 2,
            scratch_shapes=[
                pltpu.VMEM((quarter, table_width), BF),
                pltpu.VMEM((2 * count, table_width), F32),
                pltpu.SemaphoreType.DMA((1,)),
            ],
            compiler_params=limit(14),
        )(place, *parts, near_low, near_middle, near_high, in_hbm(embedding))
        got = from_peers(send, "guide", 2)[0]
        allowed = allowed_ids.shape[0]
        places = allowed_ids - (kv_index * seq_size + seq_index) * table_rows
        places = jnp.repeat(places.reshape(2, allowed // 2), group, axis=0)
        weights = lax.dynamic_slice_in_dim(guidance, guide_index * group, group, 0)
        weights = jnp.broadcast_to(jnp.concatenate([weights, weights])[:, None], (half, LANES))
        return pl.pallas_call(
            logits_kernel,
            out_shape=shape((group, allowed), F32),
            in_specs=[VMEM] * 4,
            out_specs=VMEM,
            scratch_shapes=[pltpu.VMEM((half, table_rows), F32)],
            compiler_params=limit(24),
        )(places, weights, keep, got)


def on_device(*arrays):
    units = arrays[14].shape[1] // (2 * lax.axis_size("seq"))
    requests = arrays[0].shape[1]
    if units % LANES or requests != 8 or lax.axis_size("guide") != 2:
        return plain_layer(*arrays)
    return fast_layer(*arrays)


def solution(mesh):
    return jax.shard_map(
        on_device,
        mesh=mesh,
        in_specs=(
            P(None, None, ("guide", "seq")),
            P(),
            P(),
            P(("kv", "seq")),
            P(),
            P(("guide", "seq")),
            P(("guide", "seq")),
            P(("guide", "seq")),
            P(("guide", "seq")),
            P(("guide", "seq")),
            P(("guide", "seq"), "kv"),
            P(("guide", "seq"), "kv"),
            P(("guide", "seq"), "kv"),
            P("kv", ("guide", "seq")),
            P(("guide", "seq"), "kv"),
            P(("guide", "seq"), "kv"),
            P("kv", ("guide", "seq")),
            P(("kv", "seq"), "guide"),
            P(None, ("guide", "seq"), "kv"),
            P(None, ("guide", "seq"), "kv"),
            P(None, ("guide", "seq"), "kv"),
            P(None, ("guide", "seq"), "kv"),
        ),
        out_specs=P("guide", ("kv", "seq")),
        check_vma=False,
    )
```

```python
import jax
import jax.numpy as jnp
from jax import lax
from jax.experimental import pallas as pl
from jax.experimental.pallas import tpu as pltpu
from jax.sharding import PartitionSpec as P

D = 4608
H = 32
HD = 128


EPS = 1e-06
ATTN_CAP = 50.0
LOGIT_CAP = 30.0
THETA = 10000.0
HIGHEST = lax.Precision.HIGHEST


def rotary(values, position):
    half_size = values.shape[-1] // 2
    frequency = THETA ** (-2.0 * jnp.arange(half_size, dtype=jnp.float32) / values.shape[-1])
    angles = position[:, None, None] * frequency
    first_half = values[..., :half_size]
    second_half = values[..., half_size:]
    cosine = jnp.cos(angles)
    sine_part = jnp.sin(angles)
    return jnp.concatenate(
        [
            first_half * cosine - second_half * sine_part,
            second_half * cosine + first_half * sine_part,
        ],
        axis=-1,
    )


def to_slots(slot_pick, array):
    flat = array.astype(jnp.float32).reshape(array.shape[0], array.shape[1], -1)
    moved = jnp.einsum("gsr,gre->gse", slot_pick, flat, precision=HIGHEST)
    return moved.reshape(array.shape).astype(array.dtype)


def to_requests(slot_pick, array):
    flat = array.astype(jnp.float32).reshape(array.shape[0], array.shape[1], -1)
    moved = jnp.einsum("gsr,gse->gre", slot_pick, flat, precision=HIGHEST)
    return moved.reshape(array.shape).astype(array.dtype)


def attend_block(queries, key_block, value_block, slot_len, first_pos, tile_len):
    slot_count, block_len = (key_block.shape[0], key_block.shape[1])
    local_kv, group_size, head_size = (queries.shape[1], queries.shape[2], queries.shape[3])
    live_len = jnp.clip(jnp.max(slot_len) - first_pos, 0, block_len)
    tile_count = (live_len + tile_len - 1) // tile_len

    def one_tile(tile_index, carry):
        numer, denom = carry
        tile_start = tile_index * tile_len
        key_tile = lax.dynamic_slice_in_dim(key_block, tile_start, tile_len, 1).reshape(
            slot_count, tile_len, local_kv, head_size
        )
        value_tile = lax.dynamic_slice_in_dim(value_block, tile_start, tile_len, 1).reshape(
            slot_count, tile_len, local_kv, head_size
        )
        scores = jnp.einsum(
            "rkgd,rtkd->rkgt", queries, key_tile, preferred_element_type=jnp.float32
        )
        places = first_pos + tile_start + jnp.arange(tile_len, dtype=jnp.int32)
        visible = places[None, None, None, :] < slot_len[:, None, None, None]
        probs = jnp.where(visible, jnp.exp(ATTN_CAP * jnp.tanh(scores / ATTN_CAP)), 0.0)
        numer = numer + jnp.einsum(
            "rkgt,rtkd->rkgd",
            probs.astype(jnp.bfloat16),
            value_tile,
            preferred_element_type=jnp.float32,
        )
        denom = denom + jnp.sum(probs, axis=-1)
        return (numer, denom)

    start_numer = jnp.zeros((slot_count, local_kv, group_size, head_size), jnp.float32)
    start_denom = jnp.zeros((slot_count, local_kv, group_size), jnp.float32)
    return lax.fori_loop(0, tile_count, one_tile, (start_numer, start_denom))


def plain_layer(
    hidden,
    lengths,
    slot_owner,
    allowed_ids,
    guidance,
    pre_attn_gain,
    post_attn_gain,
    pre_ffw_gain,
    post_ffw_gain,
    final_gain,
    query_weight,
    key_weight,
    value_weight,
    output_weight,
    gate_weight,
    up_weight,
    down_weight,
    embedding,
    cond_keys,
    cond_values,
    uncond_keys,
    uncond_values,
):
    kinds, requests, width_local = hidden.shape
    stream_count = kinds * requests
    local_heads = query_weight.shape[1] // HD
    local_kv = key_weight.shape[1] // HD
    group_size = local_heads // local_kv
    streams = hidden.astype(jnp.float32)
    normed = (streams * pre_attn_gain).astype(jnp.bfloat16).reshape(stream_count, width_local)
    query_part = jnp.dot(normed, query_weight, preferred_element_type=jnp.float32)
    key_part = jnp.dot(normed, key_weight, preferred_element_type=jnp.float32)
    value_part = jnp.dot(normed, value_weight, preferred_element_type=jnp.float32)
    square_part = jnp.sum(streams * streams, axis=-1)
    square_sum, query_sum, key_sum, value_sum = lax.psum(
        (square_part, query_part, key_part, value_part), ("guide", "seq")
    )
    row_scale = lax.rsqrt(square_sum / D + EPS).reshape(stream_count, 1)
    position = lengths.astype(jnp.float32).reshape(stream_count)
    queries = (
        rotary((query_sum * row_scale).reshape(stream_count, local_heads, HD), position)
        * (D // H) ** (-0.5)
    ).astype(jnp.bfloat16)
    new_keys = rotary((key_sum * row_scale).reshape(stream_count, local_kv, HD), position).astype(
        jnp.bfloat16
    )
    new_values = (value_sum * row_scale).astype(jnp.bfloat16)
    queries = queries.reshape(kinds, requests, local_kv, group_size, HD)
    new_keys = new_keys.reshape(kinds, requests, local_kv, HD)
    new_values = new_values.reshape(kinds, requests, local_kv, HD)
    matches = slot_owner[:, :, None] == jnp.arange(requests, dtype=jnp.int32)[None, None, :]
    slot_pick = matches.astype(jnp.float32)
    slot_len = jnp.sum(jnp.where(matches, lengths[:, None, :], 0), axis=-1)
    slot_queries = to_slots(slot_pick, queries)
    slot_keys = to_slots(slot_pick, new_keys)
    slot_values = to_slots(slot_pick, new_values)
    guide_index = lax.axis_index("guide")
    seq_index = lax.axis_index("seq")
    block_index = guide_index * lax.axis_size("seq") + seq_index
    cond_len = cond_keys.shape[1]
    uncond_len = uncond_keys.shape[1]
    cond_numer, cond_denom = attend_block(
        slot_queries[0],
        cond_keys,
        cond_values,
        slot_len[0],
        block_index * cond_len,
        min(256, cond_len),
    )
    uncond_numer, uncond_denom = attend_block(
        slot_queries[1],
        uncond_keys,
        uncond_values,
        slot_len[1],
        block_index * uncond_len,
        min(256, uncond_len),
    )
    numer_part = jnp.stack([cond_numer, uncond_numer])
    denom_part = jnp.stack([cond_denom, uncond_denom])
    numer_sum, denom_sum = lax.psum((numer_part, denom_part), ("guide", "seq"))
    own_score = jnp.einsum(
        "gskjd,gskd->gskj", slot_queries, slot_keys, preferred_element_type=jnp.float32
    )
    own_prob = jnp.exp(ATTN_CAP * jnp.tanh(own_score / ATTN_CAP))
    own_weight = own_prob.astype(jnp.bfloat16).astype(jnp.float32)
    numer_total = (
        numer_sum + own_weight[..., None] * slot_values.astype(jnp.float32)[:, :, :, None, :]
    )
    denom_total = denom_sum + own_prob
    attended_slots = (numer_total / denom_total[..., None]).astype(jnp.bfloat16)
    attended = to_requests(slot_pick, attended_slots).reshape(stream_count, local_heads * HD)
    out_part = jnp.dot(attended, output_weight, preferred_element_type=jnp.float32)
    projected = lax.psum(out_part, "kv").reshape(kinds, requests, width_local)
    branch_sq = lax.psum(jnp.sum(projected * projected, axis=-1), ("guide", "seq"))
    out_scale = lax.rsqrt(branch_sq / D + EPS)
    middle = streams + projected * out_scale[..., None] * post_attn_gain
    middle_sq = lax.psum(jnp.sum(middle * middle, axis=-1), ("guide", "seq"))
    ffw_in = (middle * pre_ffw_gain).astype(jnp.bfloat16).reshape(stream_count, width_local)
    ffw_scale = lax.rsqrt(middle_sq / D + EPS).reshape(stream_count, 1)
    gate_part = jnp.dot(ffw_in, gate_weight, preferred_element_type=jnp.float32)
    upward_part = jnp.dot(ffw_in, up_weight, preferred_element_type=jnp.float32)
    gate_sum, upward_sum = lax.psum((gate_part, upward_part), ("guide", "seq"))
    activ = (jax.nn.gelu(gate_sum * ffw_scale, approximate=True) * (upward_sum * ffw_scale)).astype(
        jnp.bfloat16
    )
    down_part = jnp.dot(activ, down_weight, preferred_element_type=jnp.float32)
    ffw_out = lax.psum(down_part, "kv").reshape(kinds, requests, width_local)
    ffw_sq = lax.psum(jnp.sum(ffw_out * ffw_out, axis=-1), ("guide", "seq"))
    branch_scale = lax.rsqrt(ffw_sq / D + EPS)
    last = middle + ffw_out * branch_scale[..., None] * post_ffw_gain
    last_sq = lax.psum(jnp.sum(last * last, axis=-1), ("guide", "seq"))
    final_scale = lax.rsqrt(last_sq / D + EPS)
    final_rows = (last * final_gain).astype(jnp.bfloat16)
    half_rows = lax.all_gather(final_rows, "seq", axis=2, tiled=True)
    table_rows = embedding.shape[0]
    block_first = (lax.axis_index("kv") * lax.axis_size("seq") + seq_index) * table_rows
    picked = jnp.take(embedding, allowed_ids - block_first, axis=0)
    logit_part = jnp.einsum(
        "sd,ad->sa",
        half_rows.reshape(stream_count, half_rows.shape[2]),
        picked,
        preferred_element_type=jnp.float32,
    )
    logit_term = jnp.transpose(logit_part.reshape(kinds, requests, picked.shape[0]), (1, 0, 2))
    logit_share = lax.psum_scatter(logit_term, "guide", scatter_dimension=0, tiled=True)
    half_req = requests // 2
    first_req = guide_index * half_req
    share_scale = jnp.transpose(
        lax.dynamic_slice_in_dim(final_scale, first_req, half_req, 1), (1, 0)
    )
    capped = LOGIT_CAP * jnp.tanh(logit_share * share_scale[:, :, None] / LOGIT_CAP)
    share_weight = lax.dynamic_slice_in_dim(guidance, first_req, half_req, 0)
    return capped[:, 1] + share_weight[:, None] * (capped[:, 0] - capped[:, 1])


BF = jnp.bfloat16
F32 = jnp.float32
LANES = 128
ANY = pl.BlockSpec(memory_space=pl.ANY)
VMEM = pl.BlockSpec(memory_space=pltpu.VMEM)
SMEM = pl.BlockSpec(memory_space=pltpu.SMEM)
MIB = 1 << 20
COPIES = 4
AHEAD = 5


def nt_dot(a, b):
    return lax.dot_general(a, b, (((1,), (1,)), ((), ())), preferred_element_type=F32)


def nn_dot(a, b):
    return jnp.dot(a, b, preferred_element_type=F32)


def in_hbm(value):
    return pltpu.with_memory_space_constraint(value, pltpu.HBM)


def started(sources, targets, done):
    copies = [
        pltpu.make_async_copy(source, target, done.at[at])
        for at, (source, target) in enumerate(zip(sources, targets))
    ]
    for copy in copies:
        copy.start()
    return copies


def limit(mib):
    return pltpu.CompilerParams(vmem_limit_bytes=mib * MIB)


def columns_tile(values, rows):
    lane = lax.broadcasted_iota(jnp.int32, (rows, LANES), 1)
    tile = jnp.zeros((rows, LANES), F32)
    for place, value in enumerate(values):
        tile = jnp.where(lane == place, value, tile)
    return tile


def split_tile(tile):
    high = tile.astype(BF).astype(F32)
    rest = tile - high
    middle = rest.astype(BF).astype(F32)
    low = (rest - middle).astype(BF).astype(F32)
    return (high + pltpu.roll(middle, 32, 1) + pltpu.roll(low, 64, 1)).astype(BF)


def joined_tile(tile):
    terms = tile.astype(F32)
    total = terms + pltpu.roll(terms, LANES - 32, 1) + pltpu.roll(terms, LANES - 64, 1)
    lane = lax.broadcasted_iota(jnp.int32, total.shape, 1)
    return jnp.where(lane < 32, total, 0.0)


def project_kernel(meta, *refs):
    sources, (rows, keep, send), held, done = refs[:5], refs[5:8], refs[8:13], refs[13]
    copies = started(sources, held, done)
    hidden, gain, *weights = held
    for copy in copies[:2]:
        copy.wait()
    count = hidden.shape[0]
    half = count // 2
    group = half // 2
    row = lax.broadcasted_iota(jnp.int32, (count, count), 0)
    column = lax.broadcasted_iota(jnp.int32, (count, count), 1)
    source = (row // group) % 2 * half + row // half * group + row % group
    pick = jnp.where(column == source, 1.0, 0.0).astype(BF)
    streams = nn_dot(pick, hidden[...])
    rows[...] = streams.astype(BF)
    square = jnp.sum(streams * streams, axis=-1, keepdims=True)
    normed = (streams * gain[...].reshape(1, -1)).astype(BF)
    first = meta[0] == 0
    offset = 0
    for copy, weight in zip(copies[2:], weights):
        copy.wait()
        product = nn_dot(normed, weight[...])
        width = product.shape[1] // 2
        low, high = product[:, :width], product[:, width:]
        keep[:, offset : offset + width] = jnp.where(first, low, high)
        send[:, offset : offset + width] = jnp.where(first, high, low)
        offset += width
    tile = columns_tile([square], count)
    keep[:, offset:] = tile
    send[:, offset:] = tile


def hold_kernel(starts, *refs):
    count = len(starts)
    sources, (*targets, token, done) = refs[1 : count + 1], refs[count + 1 :]
    token[...] = jnp.zeros_like(token)
    pieces = []
    for start, source, target in zip(starts, sources, targets):
        if source.shape[1:] != target.shape[1:]:
            source = source.at[:, pl.ds(0, target.shape[1])]
        size = target.shape[0] // COPIES
        pieces += [
            (source.at[pl.ds(start + at * size, size)], target.at[pl.ds(at * size, size)])
            for at in range(COPIES)
        ]
    for copy in started(*zip(*pieces), done):
        copy.wait()


def held_near(after, *values, columns=None):
    arrays = [array for array, _, _ in values]
    starts = [start for _, start, _ in values]
    shapes = [
        (rows,) + ((columns,) if columns else array.shape[1:]) for array, _, rows in values
    ]
    size = sum(2 * rows * held[-1] for (_, _, rows), held in zip(values, shapes))
    return pl.pallas_call(
        lambda *refs: hold_kernel(starts, *refs),
        out_shape=[pltpu.VMEM(held, array.dtype) for held, array in zip(shapes, arrays)]
        + [jax.ShapeDtypeStruct((8, LANES), F32)],
        in_specs=[ANY] * (1 + len(values)),
        out_specs=[VMEM] * (1 + len(values)),
        scratch_shapes=[pltpu.SemaphoreType.DMA((COPIES * len(values),))],
        cost_estimate=pl.CostEstimate(flops=0, bytes_accessed=2 * size, transcendentals=0),
        compiler_params=limit(2),
    )(after, *map(in_hbm, arrays))


def pair_kernel(keep, got, own, coded):
    total = keep[...] + got[...]
    own[...] = total
    width = total.shape[1] - LANES
    coded[:, :width] = total[:, :width].astype(BF)
    coded[:, width:] = split_tile(total[:, width:])


def added_parts(own, parts):
    width = own.shape[1] - LANES
    total, tile = own[:, :width], own[:, width:]
    for part in parts:
        total = total + part[:, :width].astype(F32)
        tile = tile + joined_tile(part[:, width:])
    return total, tile


def rope_kernel(head_dim, scale, cosine, sine, *refs):
    parts, (out, squares) = refs[:-2], refs[-2:]
    total, tile = added_parts(parts[0], parts[1:])
    blocks = total.shape[1] // head_dim
    squares[...] = tile
    row_scale = lax.rsqrt(tile[:, :1] / D + EPS)
    cosines, sines = cosine[...], sine[...]
    for block in range(blocks):
        entry = total[:, block * head_dim : (block + 1) * head_dim] * row_scale
        if block < blocks * 3 // 4:
            entry = entry * cosines + pltpu.roll(entry, head_dim // 2, 1) * sines
        if block < blocks // 2:
            entry = entry * scale
        out[:, block * head_dim : (block + 1) * head_dim] = entry.astype(BF)


def attend_kernel(meta, mine, other, *refs):
    sources, (keep, send), held = refs[:4], refs[4:6], refs[6:10]
    queries, numer, denom, done = refs[10:]
    slots = sources[0].shape[0]
    order = [(slot, which) for slot in range(slots) for which in (0, 2, 1, 3)]
    copies = started(
        [sources[which].at[slot] for slot, which in order],
        [held[which].at[slot] for slot, which in order],
        done,
    )
    arrived = dict(zip(order, copies))
    count, heads, wide = queries.shape
    head_dim = numer.shape[2]
    half = count // 2
    group = half // 2
    half_heads = heads // 2
    half_kv = half_heads // 2
    first = meta[0] == 0
    block_index = meta[1]

    def piece(index, at):
        a = mine[:, at * head_dim : (at + 1) * head_dim].astype(F32)
        b = other[:, at * head_dim : (at + 1) * head_dim].astype(F32)
        return jnp.where(first, a, b) if index == 0 else jnp.where(first, b, a)

    queries[...] = jnp.zeros_like(queries)
    for head in range(heads):
        kv = head // 2
        queries[:, head, kv * head_dim : (kv + 1) * head_dim] = piece(
            head // half_heads, head % half_heads
        )

    def place_of(kind, slot):
        request = meta[3 + (2 + kind) * half + slot]
        row = request // group * half + kind * group + request % group
        return row, meta[3 + kind * half + request]

    def scores_of(kind, slot):
        row, length = place_of(kind, slot)
        query = queries[row].astype(BF)
        scores = nt_dot(query, held[2 * kind][slot])
        place = block_index * scores.shape[1] + lax.broadcasted_iota(jnp.int32, scores.shape, 1)
        return jnp.where(
            place < length, jnp.exp(ATTN_CAP * jnp.tanh(scores / ATTN_CAP)), 0.0
        )

    head_row = lax.broadcasted_iota(jnp.int32, (heads, head_dim), 0)

    def weigh(kind, slot, probs):
        row, _ = place_of(kind, slot)
        sums = nn_dot(probs.astype(BF), held[2 * kind + 1][slot])
        folded = jnp.zeros((heads, head_dim), F32)
        for kv in range(heads // 2):
            folded = jnp.where(
                head_row // 2 == kv, sums[:, kv * head_dim : (kv + 1) * head_dim], folded
            )
        numer[row] = folded
        denom[row] = jnp.broadcast_to(
            jnp.sum(probs, axis=-1, keepdims=True), (heads, head_dim)
        )

    ready = None
    for slot in range(slots + 1):
        if slot < slots:
            arrived[slot, 0].wait()
            arrived[slot, 2].wait()
        if slot > 0:
            arrived[slot - 1, 1].wait()
            arrived[slot - 1, 3].wait()
        following = [scores_of(kind, slot) for kind in (0, 1)] if slot < slots else None
        if ready is not None:
            for kind in (0, 1):
                weigh(kind, slot - 1, ready[kind])
        ready = following

    owned = jnp.where(block_index == 0, 1.0, 0.0)
    sums, totals = [], []
    for head in range(heads):
        side = head // half_heads
        kv = head % half_heads // 2
        query = piece(side, head % half_heads)
        key = piece(side, half_heads + kv)
        value = piece(side, half_heads + half_kv + kv)
        score = jnp.sum(query * key, axis=-1, keepdims=True)
        own = jnp.exp(ATTN_CAP * jnp.tanh(score / ATTN_CAP))
        weight = own.astype(BF).astype(F32)
        sums.append(numer[:, head, :] + owned * weight * value)
        totals.append(denom[:, head, :1] + owned * own)
    for at in range(half_heads):
        low, high = sums[at], sums[half_heads + at]
        keep[:, at * head_dim : (at + 1) * head_dim] = jnp.where(first, low, high)
        send[:, at * head_dim : (at + 1) * head_dim] = jnp.where(first, high, low)
    low = columns_tile(totals[:half_heads], count)
    high = columns_tile(totals[half_heads:], count)
    keep[:, half_heads * head_dim :] = jnp.where(first, low, high)
    send[:, half_heads * head_dim :] = jnp.where(first, high, low)


def attended_kernel(*refs):
    parts, out = refs[:-1], refs[-1]
    total, tile = added_parts(parts[0], parts[1:])
    for head in range(out.shape[1] // HD):
        at = slice(head * HD, (head + 1) * HD)
        out[:, at] = (total[:, at] / tile[:, head : head + 1]).astype(BF)


def output_kernel(meta, mine, other, weight, out):
    first = meta[0] == 0
    a, b = mine[...].astype(F32), other[...].astype(F32)
    low = jnp.where(first, a, b).astype(BF)
    high = jnp.where(first, b, a).astype(BF)
    width = mine.shape[1]
    out[...] = nt_dot(low, weight[:, :width]) + nt_dot(high, weight[:, width:])


def gate_up_kernel(pieces, meta, hidden, post_gain, pre_gain, *refs):
    parts, (near_gate, gate_weight, up_weight, keep, send, branch, held, done) = refs[:-8], refs[-8:]
    count = hidden.shape[0]
    width = held.shape[2]
    guide, place = meta[0], meta[2]
    steps = 2 * pieces
    near = near_gate.shape[1] // width
    far = [(gate_weight, step) for step in range(near, steps)]
    far += [(up_weight, step) for step in range(steps)]
    copies = [
        pltpu.make_async_copy(
            weight.at[:, pl.ds(step * width, width)], held.at[at], done.at[at]
        )
        for at, (weight, step) in enumerate(far)
    ]
    for copy in copies[:AHEAD]:
        copy.start()
    projected = parts[0][...]
    for part in parts[1:]:
        projected = projected + part[...]
    streams = hidden[...].astype(F32)
    gained = projected * post_gain[...].reshape(1, -1)
    branch[...] = gained
    scale = pre_gain[...].reshape(1, -1)
    operand = jnp.concatenate([(streams * scale).astype(BF), (gained * scale).astype(BF)])
    tile = columns_tile(
        [
            jnp.sum(projected * projected, axis=-1, keepdims=True),
            jnp.sum(streams * gained, axis=-1, keepdims=True),
            jnp.sum(gained * gained, axis=-1, keepdims=True),
        ],
        count,
    )
    coded = split_tile(tile)
    for slot in range(pieces):
        keep[slot, :count, 2 * width :] = tile
        keep[slot, count:, 2 * width :] = jnp.zeros_like(tile)
        send[slot, :count, 2 * width :] = coded
        send[slot, count:, 2 * width :] = jnp.zeros_like(coded)
    for part in range(2 * steps):
        step, offset = part % steps, part // steps * width
        slot = lax.bitwise_xor(place, step % pieces)
        mine = guide == step // pieces
        if part < near:
            product = nn_dot(operand, near_gate[:, step * width : (step + 1) * width])
        else:
            copies[part - near].wait()
            if part - near + AHEAD < len(copies):
                copies[part - near + AHEAD].start()
            product = nn_dot(operand, held[part - near])

        @pl.when(mine)
        def _(product=product, slot=slot, offset=offset):
            keep[slot, :, offset : offset + width] = product

        @pl.when(jnp.logical_not(mine))
        def _(product=product, slot=slot, offset=offset):
            send[slot, :, offset : offset + width] = product.astype(BF)


def share_kernel(keep, got, own, *outs):
    width = keep.shape[2] - LANES
    count = keep.shape[1] // 2
    tile = keep[0, :count, width:] + joined_tile(got[0, :count, width:])
    own[:, :width] = keep[0, :, :width] + got[0, :, :width].astype(F32)
    own[:count, width:] = tile
    own[count:, width:] = jnp.zeros((count, LANES), F32)
    coded = split_tile(tile)
    for at, out in enumerate(outs):
        out[:, :width] = (
            keep[at + 1, :, :width] + got[at + 1, :, :width].astype(F32)
        ).astype(BF)
        out[:count, width:] = coded
        out[count:, width:] = jnp.zeros_like(coded)


def active_kernel(squares, own, *refs):
    parts, (out, scales) = refs[:-2], refs[-2:]
    count = squares.shape[0]
    width = out.shape[1]
    tile = own[:count, 2 * width :]
    for part in parts:
        tile = tile + joined_tile(part[:count, 2 * width :])
    branch_scale = lax.rsqrt(tile[:, 0:1] / D + EPS)
    middle_sq = squares[:, 0:1] + branch_scale * (
        2.0 * tile[:, 1:2] + branch_scale * tile[:, 2:3]
    )
    scale = lax.rsqrt(jnp.maximum(middle_sq, 0.0) / D + EPS)
    scales[...] = jnp.broadcast_to(branch_scale, (count, LANES))

    def summed(rows, at):
        total = own[rows, at]
        for part in parts:
            total = total + part[rows, at].astype(F32)
        return total

    low, high = slice(0, count), slice(count, 2 * count)
    gate_at, up_at = slice(0, width), slice(width, 2 * width)
    gate = (summed(low, gate_at) + branch_scale * summed(high, gate_at)) * scale
    up = (summed(low, up_at) + branch_scale * summed(high, up_at)) * scale
    out[...] = (jax.nn.gelu(gate, approximate=True) * up).astype(BF)


def by_distance(parts):
    return parts[:1] + parts[:0:-1]


def down_kernel(pieces, meta, *refs):
    parts = by_distance(refs[:pieces]) + by_distance(refs[pieces : 2 * pieces])
    weight, out = refs[2 * pieces :]
    units = parts[0].shape[1]
    guide, place = meta[0], meta[2]
    total = jnp.zeros(out.shape, F32)
    for step, part in enumerate(parts):
        side = guide if step < pieces else 1 - guide
        block = side * pieces + lax.bitwise_xor(place, step % pieces)
        held = weight[:, pl.ds(pl.multiple_of(block * units, LANES), units)]
        total = total + nt_dot(part[...], held)
    out[...] = total


def last_kernel(hidden, branch, scales, post_gain, final_gain, *refs):
    parts, out = refs[:-1], refs[-1]
    ffw = parts[0][...]
    for part in parts[1:]:
        ffw = ffw + part[...]
    count = ffw.shape[0]
    middle = hidden[...].astype(F32) + branch[...] * scales[:, 0:1]
    gained = ffw * post_gain[...].reshape(1, -1)
    scale = final_gain[...].reshape(1, -1)
    out[:count, :] = (middle * scale).astype(BF)
    out[count : 2 * count, :] = (gained * scale).astype(BF)
    tile = columns_tile(
        [
            jnp.sum(ffw * ffw, axis=-1, keepdims=True),
            jnp.sum(middle * gained, axis=-1, keepdims=True),
            jnp.sum(gained * gained, axis=-1, keepdims=True),
            jnp.sum(middle * middle, axis=-1, keepdims=True),
        ],
        count,
    )
    out[2 * count :, :LANES] = split_tile(tile)
    out[2 * count :, LANES:] = jnp.zeros((count, out.shape[1] - LANES), BF)


def table_kernel(pieces, meta, *refs):
    parts, (lower, middle, upper, table, keep, send, last, rows, done) = refs[:pieces], refs[pieces:]
    parts = by_distance(parts)
    quarter = last.shape[0]
    copies = started([table.at[pl.ds(3 * quarter, quarter)]], [last], done)
    count = parts[0].shape[0] // 3
    half = count // 2
    width = parts[0].shape[1]
    first = meta[0] == 0
    place = meta[2]
    total_rows = 4 * quarter
    for target in range(pieces):
        block = parts[0][: 2 * count, :].astype(F32)
        for at in range(1, pieces):
            block = jnp.where(
                lax.bitwise_xor(place, at) == target,
                parts[at][: 2 * count, :].astype(F32),
                block,
            )
        rows[:, target * width : (target + 1) * width] = block
    tile = joined_tile(parts[0][2 * count :, :LANES])
    for at in range(1, pieces):
        tile = tile + joined_tile(parts[at][2 * count :, :LANES])
    low, high = tile[:half], tile[half:]
    keep[:half, total_rows:] = jnp.where(first, low, high)
    send[:half, total_rows:] = jnp.where(first, high, low)
    keep[half:, total_rows:] = jnp.zeros((half, LANES), F32)
    send[half:, total_rows:] = jnp.zeros((half, LANES), F32)
    operand = rows[...].astype(BF)
    step_rows = quarter // 2
    for block in range(8):
        ref, first_row = ((lower, 0), (middle, 4), (upper, 5), (last, 6))[
            (block >= 4) + (block >= 5) + (block >= 6)
        ]
        if block == 6:
            copies[0].wait()
        start = (block - first_row) * step_rows
        product = nt_dot(ref[start : start + step_rows, :], operand).T
        at = slice(block * step_rows, (block + 1) * step_rows)
        for base in (0, half):
            low = product[2 * base : 2 * base + half]
            high = product[2 * base + half : 2 * base + 2 * half]
            keep[base : base + half, at] = jnp.where(first, low, high)
            send[base : base + half, at] = jnp.where(first, high, low)


def logits_kernel(places, weights, keep, got, out, mixed):
    rows = keep.shape[0] // 2
    group = rows // 2
    total_rows = keep.shape[1] - LANES
    tile = keep[:rows, total_rows:] + got[:rows, total_rows:]
    branch_scale = lax.rsqrt(tile[:, 0:1] / D + EPS)
    last_sq = tile[:, 3:4] + branch_scale * (
        2.0 * tile[:, 1:2] + branch_scale * tile[:, 2:3]
    )
    scale = lax.rsqrt(jnp.maximum(last_sq, 0.0) / D + EPS)
    sums = keep[:, :total_rows] + got[:, :total_rows]
    logits = LOGIT_CAP * jnp.tanh(
        (sums[:rows] + branch_scale * sums[rows:]) * scale / LOGIT_CAP
    )
    turned = pltpu.roll(logits, group, 0)
    top = lax.broadcasted_iota(jnp.int32, logits.shape, 0) < group
    uncond = jnp.where(top, turned, logits)
    cond = jnp.where(top, logits, turned)
    mixed[...] = uncond + weights[:, 0:1] * (cond - uncond)
    half = places.shape[1]
    for start in range(0, half, LANES):
        at = slice(start, start + LANES)
        wanted = places[:, at]
        lane = lax.bitwise_and(wanted, LANES - 1)
        chunk = lax.shift_right_logical(wanted, 7)
        found = jnp.zeros((rows, LANES), F32)
        for block in range(total_rows // LANES):
            values = mixed[:, block * LANES : (block + 1) * LANES]
            found = jnp.where(
                chunk == block, jnp.take_along_axis(values, lane, axis=1), found
            )
        out[:, start : start + LANES] = found[:group]
        out[:, half + start : half + start + LANES] = found[group:]


def from_peers(value, axis, size):
    values = value if isinstance(value, (list, tuple)) else [value] * (size - 1)
    return [
        lax.ppermute(values[k - 1], axis, [(i, i ^ k) for i in range(size)])
        for k in range(size - 1, 0, -1)
    ]


def pair_summed(keep, send):
    return pl.pallas_call(
        pair_kernel,
        out_shape=(
            jax.ShapeDtypeStruct(keep.shape, F32),
            jax.ShapeDtypeStruct(keep.shape, BF),
        ),
        in_specs=[VMEM] * 2,
        out_specs=(VMEM,) * 2,
        compiler_params=limit(16),
    )(keep, from_peers(send, "guide", 2)[0])


def fast_layer(
    hidden,
    lengths,
    slot_owner,
    allowed_ids,
    guidance,
    pre_attn_gain,
    post_attn_gain,
    pre_ffw_gain,
    post_ffw_gain,
    final_gain,
    query_weight,
    key_weight,
    value_weight,
    output_weight,
    gate_weight,
    up_weight,
    down_weight,
    embedding,
    cond_keys,
    cond_values,
    uncond_keys,
    uncond_values,
):
    kinds, requests, width = hidden.shape
    count = kinds * requests
    half = count // 2
    group = half // 2
    heads = query_weight.shape[1] // HD
    kv_heads = key_weight.shape[1] // HD
    seq_size = lax.axis_size("seq")
    kv_size = lax.axis_size("kv")
    guide_index = lax.axis_index("guide")
    seq_index = lax.axis_index("seq")
    kv_index = lax.axis_index("kv")
    place = jnp.stack([guide_index, guide_index * seq_size + seq_index, seq_index]).astype(jnp.int32)
    meta = jnp.concatenate(
        [
            place,
            lengths.reshape(-1),
            slot_owner.reshape(-1),
        ]
    )
    shape = jax.ShapeDtypeStruct

    position = (
        lengths.astype(F32).reshape(kinds, 2, group).transpose(1, 0, 2).reshape(count)
    )
    half_dim = HD // 2
    frequency = THETA ** (-2.0 * jnp.arange(half_dim, dtype=F32) / HD)
    angles = position[:, None] * frequency
    cosine = jnp.cos(angles)
    sine = jnp.sin(angles)
    cosine = jnp.concatenate([cosine, cosine], axis=-1)
    sine = jnp.concatenate([-sine, sine], axis=-1)

    with jax.named_scope("project"):
        joint = (heads + 2 * kv_heads) * HD // 2 + LANES
        rows, keep, send = pl.pallas_call(
            project_kernel,
            out_shape=(
                shape((count, width), BF),
                shape((count, joint), F32),
                shape((count, joint), F32),
            ),
            in_specs=[SMEM] + [ANY] * 5,
            out_specs=(VMEM,) * 3,
            scratch_shapes=[
                pltpu.VMEM(source.shape, source.dtype)
                for source in (hidden.reshape(count, width), pre_attn_gain, query_weight, key_weight, value_weight)
            ]
            + [pltpu.SemaphoreType.DMA((5,))],
            compiler_params=limit(8),
        )(place, *map(in_hbm, (hidden.reshape(count, width), pre_attn_gain, query_weight, key_weight, value_weight)))
        own, coded = pair_summed(keep, send)
        parts = [own] + from_peers(coded, "seq", seq_size)
        mine, squares = pl.pallas_call(
            lambda *refs: rope_kernel(HD, (D // H) ** (-0.5), *refs),
            out_shape=(shape((count, joint - LANES), BF), shape((count, LANES), F32)),
            in_specs=[VMEM] * (2 + seq_size),
            out_specs=(VMEM,) * 2,
            compiler_params=limit(16),
        )(cosine, sine, *parts)
        other = from_peers(mine, "guide", 2)[0]

    with jax.named_scope("attend"):
        attend_width = heads // 2 * HD + LANES
        caches = [cond_keys, cond_values, uncond_keys, uncond_values]
        keep, send = pl.pallas_call(
            attend_kernel,
            out_shape=(shape((count, attend_width), F32),) * 2,
            in_specs=[SMEM] + [VMEM] * 2 + [ANY] * 4,
            out_specs=(VMEM,) * 2,
            scratch_shapes=[pltpu.VMEM(cache.shape, cache.dtype) for cache in caches]
            + [
                pltpu.VMEM((count, heads, kv_heads * HD), F32),
                pltpu.VMEM((count, heads, HD), F32),
                pltpu.VMEM((count, heads, HD), F32),
            ]
            + [pltpu.SemaphoreType.DMA((4 * requests,))],
            compiler_params=limit(28),
        )(meta, mine, other, *map(in_hbm, caches))
        own, coded = pair_summed(keep, send)
        parts = [own] + from_peers(coded, "seq", seq_size)
        mine = pl.pallas_call(
            attended_kernel,
            out_shape=shape((count, heads // 2 * HD), BF),
            in_specs=[VMEM] * seq_size,
            out_specs=VMEM,
            compiler_params=limit(16),
        )(*parts)
        other = from_peers(mine, "guide", 2)[0]
        part = pl.pallas_call(
            output_kernel,
            out_shape=shape((count, width), F32),
            in_specs=[SMEM] + [VMEM] * 3,
            out_specs=VMEM,
            compiler_params=limit(16),
        )(place, mine, other, output_weight.T)
        parts = [part] + from_peers(part, "kv", kv_size)
        steps = 2 * seq_size
        near_steps = 5 * steps // 8
        near_gate, _ = held_near(
            part, (gate_weight, 0, width), columns=near_steps * (gate_weight.shape[1] // steps)
        )

    with jax.named_scope("gate_up"):
        hidden_units = gate_weight.shape[1]
        unit_block = hidden_units // (2 * seq_size)
        share_width = 2 * unit_block + LANES
        steps = 2 * seq_size
        keep, send, branch = pl.pallas_call(
            lambda *refs: gate_up_kernel(seq_size, *refs),
            out_shape=(
                shape((seq_size, 2 * count, share_width), F32),
                shape((seq_size, 2 * count, share_width), BF),
                shape((count, width), F32),
            ),
            in_specs=[SMEM] + [VMEM] * (4 + kv_size) + [ANY] * 2,
            out_specs=(VMEM,) * 3,
            scratch_shapes=[
                pltpu.VMEM((2 * steps - near_steps, width, unit_block), BF),
                pltpu.SemaphoreType.DMA((2 * steps - near_steps,)),
            ],
            compiler_params=limit(18),
        )(place, rows, post_attn_gain, pre_ffw_gain, *parts, near_gate, in_hbm(gate_weight), in_hbm(up_weight))
        got = from_peers(send, "guide", 2)[0]
        own, *shares = pl.pallas_call(
            share_kernel,
            out_shape=(shape((2 * count, share_width), F32),)
            + (shape((2 * count, share_width), BF),) * (seq_size - 1),
            in_specs=[VMEM] * 2,
            out_specs=(VMEM,) * seq_size,
            compiler_params=limit(16),
        )(keep, got)
        parts = from_peers(shares, "seq", seq_size)
        parts = parts[1:2] + parts[:1] + parts[2:]
        quarter = embedding.shape[0] // 4
        near_down, near_low, token = held_near(
            shares[0], (down_weight.T, 0, width), (embedding, 0, 2 * quarter)
        )
        active, scales = pl.pallas_call(
            lambda token_ref, *refs: active_kernel(*refs),
            out_shape=(shape((count, unit_block), BF), shape((count, LANES), F32)),
            in_specs=[VMEM] * (2 + seq_size),
            out_specs=(VMEM,) * 2,
            compiler_params=limit(16),
        )(token, squares, own, *parts)

    with jax.named_scope("down"):
        mine = [active] + from_peers(active, "seq", seq_size)
        other = [from_peers(value, "guide", 2)[0] for value in mine]

        part = pl.pallas_call(
            lambda *refs: down_kernel(seq_size, *refs),
            out_shape=shape((count, width), F32),
            in_specs=[SMEM] + [VMEM] * (1 + steps),
            out_specs=VMEM,
            compiler_params=limit(8),
        )(place, *mine, *other, near_down)
        parts = [part] + from_peers(part, "kv", kv_size)
        near_middle, token = held_near(part, (embedding, 2 * quarter, quarter // 2))

    with jax.named_scope("head"):
        mine = pl.pallas_call(
            lambda token_ref, *refs: last_kernel(*refs),
            out_shape=shape((3 * count, width), BF),
            in_specs=[VMEM] * (6 + kv_size),
            out_specs=VMEM,
            compiler_params=limit(16),
        )(token, rows, branch, scales, post_ffw_gain, final_gain, *parts)
        parts = [mine] + from_peers(mine, "seq", seq_size)
        near_high, _ = held_near(mine, (embedding, 5 * quarter // 2, quarter // 2))
        table_rows, table_width = embedding.shape
        keep, send = pl.pallas_call(
            lambda *refs: table_kernel(seq_size, *refs),
            out_shape=(shape((count, table_rows + LANES), F32),) * 2,
            in_specs=[SMEM] + [VMEM] * (seq_size + 3) + [ANY],
            out_specs=(VMEM,) * 2,
            scratch_shapes=[
                pltpu.VMEM((quarter, table_width), BF),
                pltpu.VMEM((2 * count, table_width), F32),
                pltpu.SemaphoreType.DMA((1,)),
            ],
            compiler_params=limit(14),
        )(place, *parts, near_low, near_middle, near_high, in_hbm(embedding))
        got = from_peers(send, "guide", 2)[0]
        allowed = allowed_ids.shape[0]
        places = allowed_ids - (kv_index * seq_size + seq_index) * table_rows
        places = jnp.repeat(places.reshape(2, allowed // 2), group, axis=0)
        weights = lax.dynamic_slice_in_dim(guidance, guide_index * group, group, 0)
        weights = jnp.broadcast_to(jnp.concatenate([weights, weights])[:, None], (half, LANES))
        return pl.pallas_call(
            logits_kernel,
            out_shape=shape((group, allowed), F32),
            in_specs=[VMEM] * 4,
            out_specs=VMEM,
            scratch_shapes=[pltpu.VMEM((half, table_rows), F32)],
            compiler_params=limit(24),
        )(places, weights, keep, got)


def on_device(*arrays):
    units = arrays[14].shape[1] // (2 * lax.axis_size("seq"))
    requests = arrays[0].shape[1]
    if units % LANES or requests != 8 or lax.axis_size("guide") != 2:
        return plain_layer(*arrays)
    return fast_layer(*arrays)


def solution(mesh):
    return jax.shard_map(
        on_device,
        mesh=mesh,
        in_specs=(
            P(None, None, ("guide", "seq")),
            P(),
            P(),
            P(("kv", "seq")),
            P(),
            P(("guide", "seq")),
            P(("guide", "seq")),
            P(("guide", "seq")),
            P(("guide", "seq")),
            P(("guide", "seq")),
            P(("guide", "seq"), "kv"),
            P(("guide", "seq"), "kv"),
            P(("guide", "seq"), "kv"),
            P("kv", ("guide", "seq")),
            P(("guide", "seq"), "kv"),
            P(("guide", "seq"), "kv"),
            P("kv", ("guide", "seq")),
            P(("kv", "seq"), "guide"),
            P(None, ("guide", "seq"), "kv"),
            P(None, ("guide", "seq"), "kv"),
            P(None, ("guide", "seq"), "kv"),
            P(None, ("guide", "seq"), "kv"),
        ),
        out_specs=P("guide", ("kv", "seq")),
        check_vma=False,
    )
```
